32 devices in a mesh: seq: 4 (over y, x), row: 8 (over z, core).
Axes of the slice: x: 2, y: 2, z: 4, core: 2. Of those that a mesh axis runs over, the one named last changes fastest.
Arguments:
- tokens: bfloat16 [2, 1024, 3072], P(None, ('seq', 'row')), may hold values from -6 to 6
- w_qkv: bfloat16 [1536, 3072], P('row'), may hold values from -0.109375 to 0.109375
- w_rate: bfloat16 [8, 3072], P('row'), may hold values from -0.109375 to 0.109375
- rate_bias: float32 [8], P('row'), may hold values from -3 to 1
- w_out: bfloat16 [512, 3072], P('row'), may hold values from -0.25 to 0.25
- w_first_init: float32 [8, 64, 256], P('row'), may hold values from -0.75 to 0.75
- b_first_init: float32 [8, 256], P('row'), may hold values from -3 to 3
- w_second_init: float32 [8, 256, 64], P('row'), may hold values from -0.375 to 0.375
- b_second_init: float32 [8, 64], P('row'), may hold values from -3 to 3
- ln_gain: float32 [8, 64], P('row'), may hold values from 0.5 to 1.5
- ln_bias: float32 [8, 64], P('row'), may hold values from -3 to 3
Outputs:
- mixed: bfloat16 [2, 1024, 3072], P(None, ('seq', 'row'))
The draws below stay inside these ranges and needn't reach their ends.
All inputs are finite; a program needn't handle non-finite values.
Results may differ from the reference program's by a relative error of at most 0.0056.
Values may be sent and summed in bfloat16 or wider, within the bound.
No kernel may reach another device: no remote copies, remote signals or barrier semaphores. Data moves between devices by JAX's collectives and lax.ppermute only.
A program may use at most 64 MiB of HBM per device.

```python
import jax
import jax.numpy as jnp
from jax import lax

D = 3072
HEAD_SIZE = 64
INNER = 256
MINI = 64
VIDEOS = 2
HEADS = 8
TOKENS = 1024


def block_scale(own_key, shape, cuts, low, top_value):
    loudness = 1.0
    for axis_at, shards_of in cuts:
        steps = jax.random.uniform(jax.random.fold_in(jax.random.fold_in(own_key, 6), axis_at), (shards_of,), jnp.float32, low / len(cuts), top_value / len(cuts))
        loudness = loudness * jnp.repeat(jnp.exp(steps), shape[axis_at] // shards_of).reshape((-1,) + (1,) * (len(shape) - 1 - axis_at))
    return loudness


def normal_values(stream_key, extent, width, bound, pieces=(), held_as=jnp.bfloat16):
    gain = block_scale(stream_key, extent, pieces, -0.22, 0.18) if pieces else 1.0
    values = jax.random.normal(stream_key, extent, jnp.float32) * width * gain
    return jnp.minimum(jnp.maximum(values, -bound), bound).astype(held_as)


def setup_inputs(seed: int = 0) -> dict:
    arg_keys = jax.random.split(jax.random.key(seed), 12)
    return {
        "tokens": normal_values(arg_keys[0], (VIDEOS, TOKENS, D), 1.0, 6.0, ((1, 32),)),
        "w_qkv": normal_values(arg_keys[1], (HEADS * 3 * HEAD_SIZE, D), D ** -0.5, 0.109375, ((0, 8),)),
        "w_rate": normal_values(arg_keys[2], (HEADS, D), D ** -0.5, 0.109375, ((0, 8),)),
        "rate_bias": jnp.clip(-3.0 + 4.0 * jax.random.uniform(arg_keys[3], (HEADS,), jnp.float32) ** block_scale(arg_keys[3], (HEADS,), ((0, 8),), -0.2, 0.2), -3.0, 1.0),
        "w_out": normal_values(arg_keys[4], (HEADS * HEAD_SIZE, D), (HEADS * HEAD_SIZE) ** -0.5, 0.25, ((0, 8),)),
        "w_first_init": normal_values(arg_keys[5], (HEADS, HEAD_SIZE, INNER), HEAD_SIZE ** -0.5, 0.75, ((0, 8),), jnp.float32),
        "b_first_init": normal_values(arg_keys[6], (HEADS, INNER), 0.5, 3.0, ((0, 8),), jnp.float32),
        "w_second_init": normal_values(arg_keys[7], (HEADS, INNER, HEAD_SIZE), INNER ** -0.5, 0.375, ((0, 8),), jnp.float32),
        "b_second_init": normal_values(arg_keys[8], (HEADS, HEAD_SIZE), 0.5, 3.0, ((0, 8),), jnp.float32),
        "ln_gain": jnp.clip(1.0 + 0.1 * jax.random.normal(arg_keys[9], (HEADS, HEAD_SIZE), jnp.float32), 0.5, 1.5),
        "ln_bias": normal_values(arg_keys[10], (HEADS, HEAD_SIZE), 0.5, 3.0, ((0, 8),), jnp.float32),
    }


gelu_coef = 0.7978845608028654
base_rate = 0.01
ln_eps = 1e-06

def gelu_tanh(entries):
    tanh_arg = gelu_coef * (entries + 0.044715 * entries * entries * entries)
    return 0.5 * entries * (1.0 + jnp.tanh(tanh_arg))

def gelu_slope(entries):
    tanh_arg = gelu_coef * (entries + 0.044715 * entries * entries * entries)
    tangent = jnp.tanh(tanh_arg)
    return 0.5 * (1.0 + tangent) + 0.5 * entries * (1.0 - tangent * tangent) * gelu_coef * (1.0 + 3.0 * 0.044715 * entries * entries)

def matmul(left, right):
    return jnp.dot(left, right, precision=lax.Precision.HIGHEST, preferred_element_type=jnp.float32)

def normalize(entries):
    centred = entries - lax.optimization_barrier(jnp.mean(entries, axis=-1, keepdims=True))
    spread = jnp.sqrt(lax.optimization_barrier(jnp.mean(centred * centred, axis=-1, keepdims=True)) + ln_eps)
    return (centred / spread, spread)

def mini_step(inner_state, batch_block, norm_gain, offset):
    w_first, b_first, w_second, b_second = inner_state
    queries, key_rows, value_rows, lr_rows = batch_block
    mini_len = queries.shape[0]
    hidden_pre = matmul(key_rows, w_first) + b_first
    hidden = gelu_tanh(hidden_pre)
    second = matmul(hidden, w_second) + b_second
    target = value_rows - key_rows
    normed, spread = normalize(second)
    grad_out = norm_gain * (norm_gain * normed + offset - target)
    feat_width = second.shape[-1]
    grad_second = (feat_width * grad_out - lax.optimization_barrier(jnp.sum(grad_out, axis=-1, keepdims=True)) - normed * lax.optimization_barrier(jnp.sum(grad_out * normed, axis=-1, keepdims=True))) / (feat_width * spread)
    grad_first = matmul(grad_second, w_second.T) * gelu_slope(hidden_pre)
    tri_mask = jnp.tril(jnp.ones((mini_len, mini_len), jnp.float32))
    eta_last = lr_rows / mini_len
    eta_table = tri_mask * eta_last[None, :]
    query_keys = matmul(queries, key_rows.T) * eta_table
    bias_first = b_first - matmul(eta_table, grad_first)
    first_bar = matmul(queries, w_first) - matmul(query_keys, grad_first) + bias_first
    hidden_bar = gelu_tanh(first_bar)
    hidden_pairs = matmul(hidden_bar, hidden.T) * eta_table
    bias_second = b_second - matmul(eta_table, grad_second)
    second_bar = matmul(hidden_bar, w_second) - matmul(hidden_pairs, grad_second) + bias_second
    w_first = w_first - matmul((key_rows * eta_last[:, None]).T, grad_first)
    b_first = b_first - matmul(eta_last[None, :], grad_first)[0]
    w_second = w_second - matmul((hidden * eta_last[:, None]).T, grad_second)
    b_second = b_second - matmul(eta_last[None, :], grad_second)[0]
    normed_bar, spread_bar = normalize(second_bar)
    result = queries + norm_gain * normed_bar + offset
    return ((w_first, b_first, w_second, b_second), result)

def run_blocks(inner_state, queries, key_rows, value_rows, lr_rows, norm_gain, offset, mini_len):
    block_count = queries.shape[0] // mini_len
    blocks = (queries.reshape(block_count, mini_len, -1), key_rows.reshape(block_count, mini_len, -1), value_rows.reshape(block_count, mini_len, -1), lr_rows.reshape(block_count, mini_len))

    def advance(loop_carry, batch_block):
        return mini_step(loop_carry, batch_block, norm_gain, offset)
    inner_state, results = lax.scan(advance, inner_state, blocks)
    return (inner_state, results.reshape(queries.shape[0], -1))

def reference(tokens, w_qkv, w_rate, rate_bias, w_out, w_first_init, b_first_init, w_second_init, b_second_init, ln_gain, ln_bias):
    flat_rows = tokens.reshape(-1, D)
    projected = lax.optimization_barrier(jnp.dot(flat_rows, w_qkv.T, preferred_element_type=jnp.float32).astype(jnp.bfloat16)).astype(jnp.float32)
    projected = projected.reshape(VIDEOS, TOKENS, HEADS, 3, HEAD_SIZE).transpose(2, 3, 0, 1, 4)
    lr_all = base_rate * jax.nn.sigmoid(jnp.dot(flat_rows, w_rate.T, preferred_element_type=jnp.float32) + rate_bias)
    lr_all = lr_all.reshape(VIDEOS, TOKENS, HEADS).transpose(2, 0, 1)

    def one_head(w_first, b_first, w_second, b_second, norm_gain, offset, queries, key_rows, value_rows, lr_rows):

        def one_video(video_q, video_k, video_v, video_lr):
            return run_blocks((w_first, b_first, w_second, b_second), video_q, video_k, video_v, video_lr, norm_gain, offset, MINI)[1]
        return jax.vmap(one_video)(queries, key_rows, value_rows, lr_rows)
    heads_all = jax.vmap(one_head)(w_first_init, b_first_init, w_second_init, b_second_init, ln_gain, ln_bias, projected[:, 0], projected[:, 1], projected[:, 2], lr_all)
    heads_out = heads_all.astype(jnp.bfloat16).transpose(1, 2, 0, 3).reshape(VIDEOS * TOKENS, HEADS * HEAD_SIZE)
    mixed = jnp.dot(heads_out, w_out, preferred_element_type=jnp.float32).astype(jnp.bfloat16)
    return mixed.reshape(VIDEOS, TOKENS, D)
```

```python
from functools import partial

import jax
import jax.numpy as jnp
from jax import lax
from jax.experimental import pallas as pl
from jax.experimental.pallas import tpu as pltpu
from jax.sharding import PartitionSpec as P

MINI = 64
gelu_coef = 0.7978845608028654
gelu_cubic = 0.044715
base_rate = 0.01
ln_eps = 1e-06

f32 = jnp.float32
bf16 = jnp.bfloat16
NN = ((1,), (0,))
NT = ((1,), (1,))
TN = ((0,), (0,))


def dot(left, right, dims=NN):
    return lax.dot_general(
        left.astype(bf16), right.astype(bf16), (dims, ((), ())), preferred_element_type=f32
    )


def lane_low(shape):
    return lax.broadcasted_iota(jnp.int32, shape, len(shape) - 1) < shape[-1] // 2


def blocks(cat):
    low = lane_low(cat.shape)
    zero = jnp.zeros_like(cat)
    return jnp.concatenate([jnp.where(low, cat, zero), jnp.where(low, zero, cat)], axis=0)


def lane_cat(rows):
    half = rows.shape[0] // 2
    return jnp.where(lane_low((half, rows.shape[1])), rows[:half], rows[half:])


def project_kernel(x_ref, w_ref, wr_ref, bias_ref, kv_ref, q_ref):
    d = w_ref.shape[0] // 3
    mini = d
    weights = jnp.concatenate(
        [w_ref[...], jnp.broadcast_to(wr_ref[...], (d, wr_ref.shape[1]))], axis=0
    )
    minis = x_ref.shape[0] // (2 * mini)
    eye = (
        lax.broadcasted_iota(jnp.int32, (2 * mini, 2 * mini), 0)
        == lax.broadcasted_iota(jnp.int32, (2 * mini, 2 * mini), 1)
    ).astype(f32)
    rates = []
    for m in range(minis):
        rows = pl.ds(m * 2 * mini, 2 * mini)
        prod = dot(x_ref[rows, :], weights, NT)
        qk, vr = prod[:, : 2 * d], prod[:, 2 * d :]
        qk_swap, vr_swap = pltpu.roll(qk, d, 1), pltpu.roll(vr, d, 1)
        low = lane_low((mini, 2 * d))
        keys = jnp.where(low, qk_swap[:mini], qk[mini:])
        queries = jnp.where(low, qk[:mini], qk_swap[mini:])
        values = jnp.where(low, vr[:mini], vr_swap[mini:])
        logits = jnp.where(lane_low(vr.shape), vr_swap, vr)
        rate = base_rate * jax.nn.sigmoid(logits + bias_ref[...]) / mini
        rates.append(jnp.sum(rate * eye, axis=0, keepdims=True))
        kv_ref[pl.ds(m * 2 * mini, mini), :] = keys.astype(bf16)
        kv_ref[pl.ds(m * 2 * mini + mini, mini), :] = values.astype(bf16)
        q_ref[pl.ds(m * mini, mini), :] = queries.astype(bf16)
    rates = jnp.concatenate(rates, axis=0)
    high = rates.astype(bf16).astype(f32)
    pad = jnp.zeros((16 - 2 * minis, 2 * d), f32)
    kv_ref[pl.ds(minis * 2 * mini, 16), :] = jnp.concatenate(
        [high, rates - high, pad], axis=0
    ).astype(bf16)


def gelu_both(z):
    square = z * z
    tangent = jnp.tanh(z * (gelu_coef + (gelu_coef * gelu_cubic) * square))
    half = 0.5 * z
    value = half + half * tangent
    slope = (0.5 + 0.5 * tangent) + (half - half * (tangent * tangent)) * (
        gelu_coef + (3.0 * gelu_coef * gelu_cubic) * square
    )
    return value, slope


def gelu(z):
    tangent = jnp.tanh(z * (gelu_coef + (gelu_coef * gelu_cubic) * (z * z)))
    half = 0.5 * z
    return half + half * tangent


def chain_kernel(
    place_ref, kv_ref, q_ref, gain_ref, bias_ref, w1_ref, b1_ref, w2_ref, b2_ref, out_ref,
    w1_s, b1_s, w2_s, b2_s, z1_s,
):
    d = w1_ref.shape[1]
    inner = w1_ref.shape[2]
    mini = d
    minis = q_ref.shape[0] // mini
    both = 2 * d
    gain = jnp.concatenate([gain_ref[...], gain_ref[...]], axis=1)
    bias = jnp.concatenate([bias_ref[...], bias_ref[...]], axis=1)
    gain_sq = gain * gain
    row_id = lax.broadcasted_iota(jnp.int32, (both, both), 0)
    lane_id = lax.broadcasted_iota(jnp.int32, (both, both), 1)
    same = ((row_id < mini) == (lane_id < mini)).astype(f32)
    causal = same * (row_id >= lane_id).astype(f32)
    ones = same.astype(bf16)
    pick = (
        lax.broadcasted_iota(jnp.int32, (mini, both), 0)
        == lax.rem(lax.broadcasted_iota(jnp.int32, (mini, both), 1), mini)
    ).astype(f32)

    def per_row(pair):
        return jnp.concatenate(
            [
                jnp.broadcast_to(pair[:1], (mini, inner)),
                jnp.broadcast_to(pair[1:], (mini, inner)),
            ],
            axis=0,
        )

    def keys_of(j, m):
        return kv_ref[j, pl.ds(m * both, mini), :]

    def step(j, m, state, z1, kb, key_cat, nxt, query):
        w1, b1, w2, b2 = state
        w1h, w2h = w1.astype(bf16), w2.astype(bf16)
        value_cat = kv_ref[j, pl.ds(m * both + mini, mini), :].astype(f32)
        rate_rows = kv_ref[j, pl.ds(minis * both, 16), :].astype(f32)
        e = dot(pick * rate_rows[m : m + 1], ones) + dot(
            pick * rate_rows[minis + m : minis + m + 1], ones
        )
        u = gain * (bias - (value_cat - key_cat.astype(f32)))
        u_mean = dot(u, ones) * (1.0 / d)

        x2, slope = gelu_both(z1)
        x2h = x2.astype(bf16)
        z = lane_cat(dot(x2h, w2h, NT)) + b2
        zz = z * z
        sums = dot(
            jnp.concatenate([zz, gain_sq * z, gain_sq * zz, u * z], axis=0), ones
        ) * (1.0 / d)
        rs = lax.rsqrt(sums[:mini] + ln_eps)
        mean_g = rs * sums[mini : 2 * mini] + u_mean
        mean_gn = rs * (rs * sums[2 * mini : 3 * mini] + sums[3 * mini :])
        h2 = (e * rs) * ((gain_sq * rs - rs * mean_gn) * z + (u - mean_g))
        h2h = blocks(h2).astype(bf16)
        h1 = dot(h2h, w2h) * slope
        h1h = h1.astype(bf16)

        z1_next, kb_next = None, None
        if nxt is not None:
            kb_next = blocks(nxt)
            cross = dot(kb_next, kb, NT) + same
            z1_next = dot(kb_next, w1h) + per_row(b1) - dot(cross, h1h)

        result = None
        if query is not None:
            qb = blocks(query)
            attend = causal * (dot(qb, kb, NT) + 1.0)
            first_bar = dot(qb, w1h) + per_row(b1) - dot(attend, h1h)
            hidden_bar = gelu(first_bar).astype(bf16)
            attend_hidden = causal * (dot(hidden_bar, x2h, NT) + 1.0)
            zb = lane_cat(dot(hidden_bar, w2h, NT) - dot(attend_hidden, h2h)) + b2
            var = dot(zb * zb, ones) * (1.0 / d)
            result = query.astype(f32) + gain * (zb * lax.rsqrt(var + ln_eps)) + bias

        w1 = w1 - dot(kb, h1h, TN)
        b1 = b1 - jnp.concatenate(
            [
                jnp.sum(h1[:mini], axis=0, keepdims=True),
                jnp.sum(h1[mini:], axis=0, keepdims=True),
            ],
            axis=0,
        )
        w2 = w2 - dot(h2h, x2h, TN)
        b2 = b2 - jnp.sum(h2, axis=0, keepdims=True)
        return (w1, b1, w2, b2), z1_next, kb_next, result

    def load():
        return w1_s[...], b1_s[...], w2_s[...], b2_s[...]

    def store(state):
        w1_s[...], b1_s[...], w2_s[...], b2_s[...] = state

    first = w1_ref[0]
    w1 = jnp.concatenate([first, first], axis=0)
    b1 = jnp.concatenate([b1_ref[...], b1_ref[...]], axis=0)
    second = w2_ref[0]
    second = second - jnp.mean(second, axis=1, keepdims=True)
    w2 = jnp.concatenate([second, second], axis=1).T
    b2 = b2_ref[...]
    b2 = b2 - jnp.mean(b2, axis=1, keepdims=True)
    b2 = jnp.concatenate([b2, b2], axis=1)
    store((w1, b1, w2, b2))
    z1_s[...] = dot(blocks(keys_of(0, 0)), w1) + per_row(b1)
    place = place_ref[0]

    def segment(j, carry):
        state, z1 = load(), z1_s[...]
        key_cat = keys_of(j, 0)
        kb = blocks(key_cat)
        for m in range(minis):
            nxt = keys_of(j, m + 1) if m + 1 < minis else keys_of(j + 1, 0)
            state, z1, kb, _ = step(j, m, state, z1, kb, key_cat, nxt, None)
            key_cat = nxt
        store(state)
        z1_s[...] = z1
        return carry

    lax.fori_loop(0, place, segment, 0)

    state, z1 = load(), z1_s[...]
    key_cat = keys_of(place, 0)
    kb = blocks(key_cat)
    for m in range(minis):
        nxt = keys_of(place, m + 1) if m + 1 < minis else None
        query = q_ref[pl.ds(m * mini, mini), :]
        state, z1, kb, result = step(place, m, state, z1, kb, key_cat, nxt, query)
        out_ref[pl.ds(m * mini, mini), :] = result.astype(bf16)
        key_cat = nxt


def out_kernel(heads_ref, w_ref, out_ref):
    heads, rows, both = heads_ref.shape
    d = both // 2
    low = lane_low((rows, both))
    firsts, seconds = [], []
    for h in range(0, heads, 2):
        even, odd = heads_ref[h].astype(f32), heads_ref[h + 1].astype(f32)
        firsts.append(jnp.where(low, even, pltpu.roll(odd, d, 1)))
        seconds.append(jnp.where(low, pltpu.roll(even, d, 1), odd))
    lhs = jnp.concatenate(
        [jnp.concatenate(firsts, axis=1), jnp.concatenate(seconds, axis=1)], axis=0
    )
    prod = dot(lhs, w_ref[...]).astype(bf16)
    out_ref[0] = prod[:rows]
    out_ref[1] = prod[rows:]


VMEM_LIMIT = 56 * 1024 * 1024


def on_device(
    tokens,
    w_qkv,
    w_rate,
    rate_bias,
    w_out,
    w_first_init,
    b_first_init,
    w_second_init,
    b_second_init,
    ln_gain,
    ln_bias,
):
    videos, tok_part, width = tokens.shape
    d = w_qkv.shape[0] // 3
    row_count = lax.axis_size("row")
    seg = tok_part * row_count
    minis = seg // MINI
    full_out = lax.all_gather(w_out, "row", axis=0, tiled=True)
    gathered = lax.all_gather(tokens, "row", axis=1, tiled=True)
    x = gathered.reshape(videos, minis, MINI, width).transpose(1, 0, 2, 3).reshape(-1, width)
    vmem = pl.BlockSpec(memory_space=pltpu.VMEM)
    smem = pl.BlockSpec(memory_space=pltpu.SMEM)
    params = pltpu.CompilerParams(vmem_limit_bytes=VMEM_LIMIT)
    kv, q = pl.pallas_call(
        project_kernel,
        out_shape=(
            jax.ShapeDtypeStruct((minis * 2 * MINI + 16, 2 * d), bf16),
            jax.ShapeDtypeStruct((minis * MINI, 2 * d), bf16),
        ),
        in_specs=[vmem] * 4,
        out_specs=(vmem, vmem),
        compiler_params=params,
        name="project",
    )(x, w_qkv, w_rate, rate_bias.reshape(1, 1))
    kv_all = lax.all_gather(kv, "seq")
    place = lax.axis_index("seq").astype(jnp.int32).reshape(1)
    inner = w_first_init.shape[2]
    heads = pl.pallas_call(
        chain_kernel,
        out_shape=jax.ShapeDtypeStruct((minis * MINI, 2 * d), bf16),
        in_specs=[smem] + [vmem] * 8,
        out_specs=vmem,
        scratch_shapes=[
            pltpu.VMEM((2 * d, inner), f32),
            pltpu.VMEM((2, inner), f32),
            pltpu.VMEM((2 * d, inner), f32),
            pltpu.VMEM((1, 2 * d), f32),
            pltpu.VMEM((2 * MINI, inner), f32),
        ],
        compiler_params=params,
        name="chain",
    )(place, kv_all, q, ln_gain, ln_bias, w_first_init, b_first_init, w_second_init, b_second_init)
    heads = heads.reshape(row_count, tok_part, 2 * d)
    arrived = lax.all_to_all(heads, "row", split_axis=0, concat_axis=0, tiled=True)
    return pl.pallas_call(
        out_kernel,
        out_shape=jax.ShapeDtypeStruct((videos, tok_part, width), bf16),
        in_specs=[vmem, vmem],
        out_specs=vmem,
        compiler_params=params,
        name="mix",
    )(arrived, full_out)


def solution(mesh):
    in_specs = (
        P(None, ("seq", "row"), None),
        P("row", None),
        P("row", None),
        P("row"),
        P("row", None),
        P("row", None, None),
        P("row", None),
        P("row", None, None),
        P("row", None),
        P("row", None),
        P("row", None),
    )
    out_specs = P(None, ("seq", "row"), None)
    return jax.shard_map(
        on_device, mesh=mesh, in_specs=in_specs, out_specs=out_specs, check_vma=False
    )
```

```python
from functools import partial

import jax
import jax.numpy as jnp
from jax import lax
from jax.experimental import pallas as pl
from jax.experimental.pallas import tpu as pltpu
from jax.sharding import PartitionSpec as P

MINI = 64
gelu_coef = 0.7978845608028654
gelu_cubic = 0.044715
base_rate = 0.01
ln_eps = 1e-06

f32 = jnp.float32
bf16 = jnp.bfloat16
NN = ((1,), (0,))
NT = ((1,), (1,))
TN = ((0,), (0,))


def passed_along(array, axis, by):
    size = lax.axis_size(axis)
    return lax.ppermute(array, axis, [(i, i + by) for i in range(size - by)])


def dot(left, right, dims=NN):
    return lax.dot_general(
        left.astype(bf16), right.astype(bf16), (dims, ((), ())), preferred_element_type=f32
    )


def lane_low(shape):
    return lax.broadcasted_iota(jnp.int32, shape, len(shape) - 1) < shape[-1] // 2


def blocks(cat):
    low = lane_low(cat.shape)
    zero = jnp.zeros_like(cat)
    return jnp.concatenate([jnp.where(low, cat, zero), jnp.where(low, zero, cat)], axis=0)


def lane_cat(rows):
    half = rows.shape[0] // 2
    return jnp.where(lane_low((half, rows.shape[1])), rows[:half], rows[half:])


def project_kernel(count, *refs):
    x_refs, (w_ref, wr_ref, prod_ref, stack_ref) = refs[:count], refs[count:]
    d = w_ref.shape[0] // 3
    stack_ref[: 3 * d, :] = w_ref[...]
    stack_ref[3 * d :, :] = jnp.broadcast_to(wr_ref[...], (d, wr_ref.shape[1]))
    x = jnp.concatenate([x_ref[...].reshape(-1, x_ref.shape[2]) for x_ref in x_refs], axis=0)
    prod_ref[...] = dot(x, stack_ref[...], NT)


def finish_kernel(count, part, spots_ref, early_ref, *refs):
    x_refs, (stack_ref, bias_ref, kv_ref, q_ref, prod_s) = refs[:count], refs[count:]
    mini = stack_ref.shape[0] // 4
    x = jnp.concatenate([x_ref[...].reshape(-1, x_ref.shape[2]) for x_ref in x_refs], axis=0)
    late = dot(x, stack_ref[...], NT)
    early_count = early_ref.shape[0] // (2 * part)
    for i in range(early_count + count):
        spot = pl.multiple_of(spots_ref[i], part)
        for video in range(2):
            row = (2 * i + video) * part
            if i < early_count:
                prod = early_ref[pl.ds(row, part), :]
            else:
                row -= early_ref.shape[0]
                prod = late[row : row + part]
            prod_s[pl.ds(spot + video * mini, part), :] = prod
    pack(prod_s, bias_ref, kv_ref, q_ref, mini)


def pack(prod_s, bias_ref, kv_ref, q_ref, mini):
    d = prod_s.shape[1] // 4
    minis = prod_s.shape[0] // (2 * mini)
    eye = (
        lax.broadcasted_iota(jnp.int32, (2 * mini, 2 * mini), 0)
        == lax.broadcasted_iota(jnp.int32, (2 * mini, 2 * mini), 1)
    ).astype(f32)
    rates = []
    for m in range(minis):
        prod = prod_s[pl.ds(m * 2 * mini, 2 * mini), :]
        qk, vr = prod[:, : 2 * d], prod[:, 2 * d :]
        qk_swap, vr_swap = pltpu.roll(qk, d, 1), pltpu.roll(vr, d, 1)
        low = lane_low((mini, 2 * d))
        keys = jnp.where(low, qk_swap[:mini], qk[mini:])
        queries = jnp.where(low, qk[:mini], qk_swap[mini:])
        values = jnp.where(low, vr[:mini], vr_swap[mini:])
        logits = jnp.where(lane_low(vr.shape), vr_swap, vr)
        rate = base_rate * jax.nn.sigmoid(logits + bias_ref[...]) / mini
        rates.append(jnp.sum(rate * eye, axis=0, keepdims=True))
        kv_ref[pl.ds(m * 2 * mini, mini), :] = keys.astype(bf16)
        kv_ref[pl.ds(m * 2 * mini + mini, mini), :] = values.astype(bf16)
        q_ref[pl.ds(m * mini, mini), :] = queries.astype(bf16)
    rates = jnp.concatenate(rates, axis=0)
    high = rates.astype(bf16).astype(f32)
    pad = jnp.zeros((16 - 2 * minis, 2 * d), f32)
    kv_ref[pl.ds(minis * 2 * mini, 16), :] = jnp.concatenate(
        [high, rates - high, pad], axis=0
    ).astype(bf16)


def gelu_both(z):
    square = z * z
    tangent = jnp.tanh(z * (gelu_coef + (gelu_coef * gelu_cubic) * square))
    half = 0.5 * z
    value = half + half * tangent
    slope = (0.5 + 0.5 * tangent) + (half - half * (tangent * tangent)) * (
        gelu_coef + (3.0 * gelu_coef * gelu_cubic) * square
    )
    return value, slope


def gelu(z):
    tangent = jnp.tanh(z * (gelu_coef + (gelu_coef * gelu_cubic) * (z * z)))
    half = 0.5 * z
    return half + half * tangent


def chain_kernel(seq_count, place_ref, *refs):
    kv_refs, refs = refs[:seq_count], refs[seq_count:]
    q_ref, gain_ref, bias_ref, w1_ref, b1_ref, w2_ref, b2_ref, out_ref = refs[:8]
    kv_ref, w1_s, b1_s, w2_s, b2_s, z1_s = refs[8:]
    place = place_ref[0]
    for back in range(seq_count):

        @pl.when(place >= back)
        def _(back=back):
            kv_ref[place - back] = kv_refs[back][...]

    d = w1_ref.shape[1]
    inner = w1_ref.shape[2]
    mini = d
    minis = q_ref.shape[0] // mini
    both = 2 * d
    gain = jnp.concatenate([gain_ref[...], gain_ref[...]], axis=1)
    bias = jnp.concatenate([bias_ref[...], bias_ref[...]], axis=1)
    gain_sq = gain * gain
    row_id = lax.broadcasted_iota(jnp.int32, (both, both), 0)
    lane_id = lax.broadcasted_iota(jnp.int32, (both, both), 1)
    same = ((row_id < mini) == (lane_id < mini)).astype(f32)
    causal = same * (row_id >= lane_id).astype(f32)
    ones = same.astype(bf16)
    pick = (
        lax.broadcasted_iota(jnp.int32, (mini, both), 0)
        == lax.rem(lax.broadcasted_iota(jnp.int32, (mini, both), 1), mini)
    ).astype(f32)

    def per_row(pair):
        return jnp.concatenate(
            [
                jnp.broadcast_to(pair[:1], (mini, inner)),
                jnp.broadcast_to(pair[1:], (mini, inner)),
            ],
            axis=0,
        )

    def keys_of(j, m):
        return kv_ref[j, pl.ds(m * both, mini), :]

    def step(j, m, state, z1, kb, key_cat, nxt, query):
        w1, b1, w2, b2 = state
        w1h, w2h = w1.astype(bf16), w2.astype(bf16)
        value_cat = kv_ref[j, pl.ds(m * both + mini, mini), :].astype(f32)
        rate_rows = kv_ref[j, pl.ds(minis * both, 16), :].astype(f32)
        e = dot(pick * rate_rows[m : m + 1], ones) + dot(
            pick * rate_rows[minis + m : minis + m + 1], ones
        )
        u = gain * (bias - (value_cat - key_cat.astype(f32)))
        u_mean = dot(u, ones) * (1.0 / d)

        x2, slope = gelu_both(z1)
        x2h = x2.astype(bf16)
        z = lane_cat(dot(x2h, w2h, NT)) + b2
        zz = z * z
        sums = dot(
            jnp.concatenate([zz, gain_sq * z, gain_sq * zz, u * z], axis=0), ones
        ) * (1.0 / d)
        rs = lax.rsqrt(sums[:mini] + ln_eps)
        mean_g = rs * sums[mini : 2 * mini] + u_mean
        mean_gn = rs * (rs * sums[2 * mini : 3 * mini] + sums[3 * mini :])
        h2 = (e * rs) * ((gain_sq * rs - rs * mean_gn) * z + (u - mean_g))
        h2h = blocks(h2).astype(bf16)
        h1 = dot(h2h, w2h) * slope
        h1h = h1.astype(bf16)

        z1_next, kb_next = None, None
        if nxt is not None:
            kb_next = blocks(nxt)
            cross = dot(kb_next, kb, NT) + same
            z1_next = dot(kb_next, w1h) + per_row(b1) - dot(cross, h1h)

        result = None
        if query is not None:
            qb = blocks(query)
            attend = causal * (dot(qb, kb, NT) + 1.0)
            first_bar = dot(qb, w1h) + per_row(b1) - dot(attend, h1h)
            hidden_bar = gelu(first_bar).astype(bf16)
            attend_hidden = causal * (dot(hidden_bar, x2h, NT) + 1.0)
            zb = lane_cat(dot(hidden_bar, w2h, NT) - dot(attend_hidden, h2h)) + b2
            var = dot(zb * zb, ones) * (1.0 / d)
            result = query.astype(f32) + gain * (zb * lax.rsqrt(var + ln_eps)) + bias

        w1 = w1 - dot(kb, h1h, TN)
        b1 = b1 - jnp.concatenate(
            [
                jnp.sum(h1[:mini], axis=0, keepdims=True),
                jnp.sum(h1[mini:], axis=0, keepdims=True),
            ],
            axis=0,
        )
        w2 = w2 - dot(h2h, x2h, TN)
        b2 = b2 - jnp.sum(h2, axis=0, keepdims=True)
        return (w1, b1, w2, b2), z1_next, kb_next, result

    def load():
        return w1_s[...], b1_s[...], w2_s[...], b2_s[...]

    def store(state):
        w1_s[...], b1_s[...], w2_s[...], b2_s[...] = state

    first = w1_ref[0]
    w1 = jnp.concatenate([first, first], axis=0)
    b1 = jnp.concatenate([b1_ref[...], b1_ref[...]], axis=0)
    second = w2_ref[0]
    second = second - jnp.mean(second, axis=1, keepdims=True)
    w2 = jnp.concatenate([second, second], axis=1).T
    b2 = b2_ref[...]
    b2 = b2 - jnp.mean(b2, axis=1, keepdims=True)
    b2 = jnp.concatenate([b2, b2], axis=1)
    store((w1, b1, w2, b2))
    z1_s[...] = dot(blocks(keys_of(0, 0)), w1) + per_row(b1)

    def segment(j, carry):
        state, z1 = load(), z1_s[...]
        key_cat = keys_of(j, 0)
        kb = blocks(key_cat)
        for m in range(minis):
            nxt = keys_of(j, m + 1) if m + 1 < minis else keys_of(j + 1, 0)
            state, z1, kb, _ = step(j, m, state, z1, kb, key_cat, nxt, None)
            key_cat = nxt
        store(state)
        z1_s[...] = z1
        return carry

    lax.fori_loop(0, place, segment, 0)

    state, z1 = load(), z1_s[...]
    key_cat = keys_of(place, 0)
    kb = blocks(key_cat)
    for m in range(minis):
        nxt = keys_of(place, m + 1) if m + 1 < minis else None
        query = q_ref[pl.ds(m * mini, mini), :]
        state, z1, kb, result = step(place, m, state, z1, kb, key_cat, nxt, query)
        out_ref[pl.ds(m * mini, mini), :] = result.astype(bf16)
        key_cat = nxt


def out_kernel(count, owners_ref, heads_ref, *refs):
    w_refs, out_ref = refs[:count], refs[count]
    _, rows, both = heads_ref.shape
    d = both // 2
    low = lane_low((rows, both))
    firsts, seconds = [], []
    per = heads_ref.shape[0] // count
    order = [owners_ref[i] * per + j for i in range(count) for j in range(per)]
    for h in range(0, len(order), 2):
        even, odd = heads_ref[order[h]].astype(f32), heads_ref[order[h + 1]].astype(f32)
        firsts.append(jnp.where(low, even, pltpu.roll(odd, d, 1)))
        seconds.append(jnp.where(low, pltpu.roll(even, d, 1), odd))
    lhs = jnp.concatenate(
        [jnp.concatenate(firsts, axis=1), jnp.concatenate(seconds, axis=1)], axis=0
    )
    weights = jnp.concatenate([w_ref[...] for w_ref in w_refs], axis=0)
    prod = dot(lhs, weights).astype(bf16)
    out_ref[0] = prod[:rows]
    out_ref[1] = prod[rows:]


def swapped(array, flip):
    return lax.ppermute(array, "row", [(i, i ^ flip) for i in range(lax.axis_size("row"))])


VMEM_LIMIT = 56 * 1024 * 1024


def on_device(
    tokens,
    w_qkv,
    w_rate,
    rate_bias,
    w_out,
    w_first_init,
    b_first_init,
    w_second_init,
    b_second_init,
    ln_gain,
    ln_bias,
):
    videos, tok_part, width = tokens.shape
    d = w_qkv.shape[0] // 3
    row_count = lax.axis_size("row")
    seg = tok_part * row_count
    minis = seg // MINI
    vmem = pl.BlockSpec(memory_space=pltpu.VMEM)
    smem = pl.BlockSpec(memory_space=pltpu.SMEM)
    params = pltpu.CompilerParams(vmem_limit_bytes=VMEM_LIMIT)
    row = lax.axis_index("row")
    if row_count == 8:
        far, near, own = lax.optimization_barrier(
            (swapped(tokens, 4), swapped(tokens, 2), swapped(tokens, 1))
        )
        last = swapped(far, 2)
        early = [tokens, own, far, swapped(far, 1), near, swapped(near, 1)]
        owners = [row ^ flip for flip in (0, 1, 4, 5, 2, 3, 6, 7)]
        w_owners = jnp.stack(owners).astype(jnp.int32)
    else:
        whole = lax.all_gather(tokens, "row", axis=1, tiled=True)
        whole = whole.reshape(videos, minis, MINI, width)
        parts = [whole[:, m] for m in range(minis)]
        early, late = parts[:-1], parts[-1:]
        owners = [m * (MINI // tok_part) for m in range(minis)]
        w_parts = [lax.all_gather(w_out, "row", axis=0, tiled=True)]
        w_owners = jnp.zeros((1,), jnp.int32)
    per_mini = MINI // tok_part
    spots = jnp.stack(
        [
            jnp.int32((o // per_mini) * (2 * MINI) + (o % per_mini) * tok_part) for o in owners
        ]
    )
    part = early[0].shape[1]
    early_prod, stack = pl.pallas_call(
        partial(project_kernel, len(early)),
        out_shape=(
            jax.ShapeDtypeStruct((len(early) * 2 * part, 4 * d), f32),
            jax.ShapeDtypeStruct((4 * d, width), bf16),
        ),
        in_specs=[vmem] * (len(early) + 2),
        out_specs=(vmem, vmem),
        compiler_params=params,
        cost_estimate=pl.CostEstimate(
            flops=len(early) * 4 * part * 4 * d * width, bytes_accessed=3_600_000, transcendentals=0
        ),
        name="project",
    )(*early, w_qkv, w_rate)
    if row_count == 8:
        last, early_prod = lax.optimization_barrier((last, early_prod))
        late = [last, swapped(last, 1)]
        w_after, _ = lax.optimization_barrier((w_out, last))
        w_parts = [w_out] + [swapped(w_after, flip) for flip in (4, 2, 6)]
    kv, q = pl.pallas_call(
        partial(finish_kernel, len(late), part),
        out_shape=(
            jax.ShapeDtypeStruct((minis * 2 * MINI + 16, 2 * d), bf16),
            jax.ShapeDtypeStruct((minis * MINI, 2 * d), bf16),
        ),
        in_specs=[smem] + [vmem] * (len(late) + 3),
        out_specs=(vmem, vmem),
        scratch_shapes=[pltpu.VMEM((minis * 2 * MINI, 4 * d), f32)],
        compiler_params=params,
        name="finish",
    )(spots, early_prod, *late, stack, rate_bias.reshape(1, 1))
    seq_count = lax.axis_size("seq")
    place = lax.axis_index("seq").astype(jnp.int32).reshape(1)
    kvs = [kv] + [None] * (seq_count - 1)
    for back in range(seq_count - 1, 0, -1):
        kvs[back] = passed_along(kv, "seq", back)
    inner = w_first_init.shape[2]
    heads = pl.pallas_call(
        partial(chain_kernel, seq_count),
        out_shape=jax.ShapeDtypeStruct((minis * MINI, 2 * d), bf16),
        in_specs=[smem] + [vmem] * (seq_count + 7),
        out_specs=vmem,
        scratch_shapes=[
            pltpu.VMEM((seq_count,) + kv.shape, bf16),
            pltpu.VMEM((2 * d, inner), f32),
            pltpu.VMEM((2, inner), f32),
            pltpu.VMEM((2 * d, inner), f32),
            pltpu.VMEM((1, 2 * d), f32),
            pltpu.VMEM((2 * MINI, inner), f32),
        ],
        compiler_params=params,
        name="chain",
    )(place, *kvs, q, ln_gain, ln_bias, w_first_init, b_first_init, w_second_init, b_second_init)
    heads = heads.reshape(row_count, tok_part, 2 * d)
    if row_count == 8:
        w_parts = lax.optimization_barrier((heads, *w_parts))[1:]
        w_parts = [x for w in w_parts for x in (w, swapped(w, 1))]
    arrived = lax.all_to_all(heads, "row", split_axis=0, concat_axis=0, tiled=True)
    return pl.pallas_call(
        partial(out_kernel, len(w_parts)),
        out_shape=jax.ShapeDtypeStruct((videos, tok_part, width), bf16),
        in_specs=[smem, vmem] + [vmem] * len(w_parts),
        out_specs=vmem,
        compiler_params=params,
        name="mix",
    )(w_owners, arrived, *w_parts)


def solution(mesh):
    in_specs = (
        P(None, ("seq", "row"), None),
        P("row", None),
        P("row", None),
        P("row"),
        P("row", None),
        P("row", None, None),
        P("row", None),
        P("row", None, None),
        P("row", None),
        P("row", None),
        P("row", None),
    )
    out_specs = P(None, ("seq", "row"), None)
    return jax.shard_map(
        on_device, mesh=mesh, in_specs=in_specs, out_specs=out_specs, check_vma=False
    )
```

```python
from functools import partial

import jax
import jax.numpy as jnp
from jax import lax
from jax.experimental import pallas as pl
from jax.experimental.pallas import tpu as pltpu
from jax.sharding import PartitionSpec as P

MINI = 64
gelu_coef = 0.7978845608028654
gelu_cubic = 0.044715
base_rate = 0.01
ln_eps = 1e-06

f32 = jnp.float32
bf16 = jnp.bfloat16
NN = ((1,), (0,))
NT = ((1,), (1,))
TN = ((0,), (0,))


def dot(left, right, dims=NN):
    return lax.dot_general(
        left.astype(bf16), right.astype(bf16), (dims, ((), ())), preferred_element_type=f32
    )


def lane_low(shape):
    return lax.broadcasted_iota(jnp.int32, shape, len(shape) - 1) < shape[-1] // 2


def blocks(cat):
    low = lane_low(cat.shape)
    zero = jnp.zeros_like(cat)
    return jnp.concatenate([jnp.where(low, cat, zero), jnp.where(low, zero, cat)], axis=0)


def lane_cat(rows):
    half = rows.shape[0] // 2
    return jnp.where(lane_low((half, rows.shape[1])), rows[:half], rows[half:])


PACK = 16


def project_kernel(count, pieces, first, ids_ref, *refs):
    x_refs, refs = refs[: count * pieces], refs[count * pieces :]
    if first:
        w_ref, wr_ref, bias_ref, kv_ref, q_ref, stack_ref, prod_s = refs
        d, base = w_ref.shape[0] // 3, 0
        stack_ref[: 3 * d, :] = w_ref[...]
        stack_ref[3 * d :, :] = jnp.broadcast_to(wr_ref[...], (d, wr_ref.shape[1]))
    else:
        stack_ref, bias_ref, early_ref, kv_ref, q_ref, prod_s = refs
        d = stack_ref.shape[0] // 4
        base = early_ref.shape[0]
        kv_ref[:base, :] = early_ref[...]
    mini = d
    both = 2 * mini
    part = x_refs[0].shape[1]
    x = jnp.concatenate([x_ref[...].reshape(-1, x_ref.shape[2]) for x_ref in x_refs], axis=0)
    prod = dot(x, stack_ref[...], NT)
    core = ids_ref[2]
    for i in range(count):
        for j in range(pieces):
            where = (core if j == 0 else 1 - core) * part if pieces > 1 else 0
            for video in range(2):
                row = ((i * pieces + j) * 2 + video) * part
                spot = i * both + video * mini + where
                if pieces > 1:
                    spot = pl.multiple_of(spot, part)
                prod_s[pl.ds(spot, part), :] = prod[row : row + part]
    eye = (
        lax.broadcasted_iota(jnp.int32, (both, both), 0)
        == lax.broadcasted_iota(jnp.int32, (both, both), 1)
    ).astype(f32)
    low = lane_low((mini, 2 * d))
    for i in range(count):
        prod = prod_s[pl.ds(i * both, both), :]
        qk, vr = prod[:, : 2 * d], prod[:, 2 * d :]
        qk_swap, vr_swap = pltpu.roll(qk, d, 1), pltpu.roll(vr, d, 1)
        keys = jnp.where(low, qk_swap[:mini], qk[mini:])
        queries = jnp.where(low, qk[:mini], qk_swap[mini:])
        values = jnp.where(low, vr[:mini], vr_swap[mini:])
        logits = jnp.where(lane_low(vr.shape), vr_swap, vr)
        logits = jnp.sum(logits * eye, axis=0, keepdims=True)
        rate = base_rate * jax.nn.sigmoid(logits + bias_ref[...]) / mini
        high = rate.astype(bf16).astype(f32)
        pad = jnp.zeros((PACK - 2, both), f32)
        at = base + i * (both + PACK)
        kv_ref[pl.ds(at, mini), :] = keys.astype(bf16)
        kv_ref[pl.ds(at + mini, mini), :] = values.astype(bf16)
        kv_ref[pl.ds(at + both, PACK), :] = jnp.concatenate([high, rate - high, pad], axis=0).astype(bf16)
        q_ref[pl.ds(i * mini, mini), :] = queries.astype(bf16)


def gelu_both(z):
    square = z * z
    tangent = jnp.tanh(z * (gelu_coef + (gelu_coef * gelu_cubic) * square))
    half = 0.5 * z
    value = half + half * tangent
    slope = (0.5 + 0.5 * tangent) + (half - half * (tangent * tangent)) * (
        gelu_coef + (3.0 * gelu_coef * gelu_cubic) * square
    )
    return value, slope


def gelu(z):
    tangent = jnp.tanh(z * (gelu_coef + (gelu_coef * gelu_cubic) * (z * z)))
    half = 0.5 * z
    return half + half * tangent


def chain_kernel(seq_count, ids_ref, *refs):
    kv_ref, refs = refs[0], refs[1:]
    q_early, q_late, gain_ref, bias_ref, w1_ref, b1_ref, w2_ref, b2_ref = refs[:8]
    out_ref, kv_s, q_s, w1_s, b1_s, w2_s, b2_s, z1_s = refs[8:]
    inner = w1_ref.shape[-1]
    both = gain_ref.shape[1] * 2
    d = both // 2
    mini = d
    minis = kv_s.shape[1]
    place, flip = ids_ref[0], ids_ref[1]
    gain = jnp.concatenate([gain_ref[...], gain_ref[...]], axis=1)
    bias = jnp.concatenate([bias_ref[...], bias_ref[...]], axis=1)
    gain_sq = gain * gain
    row_id = lax.broadcasted_iota(jnp.int32, (both, both), 0)
    lane_id = lax.broadcasted_iota(jnp.int32, (both, both), 1)
    same = ((row_id < mini) == (lane_id < mini)).astype(f32)
    causal = same * (row_id >= lane_id).astype(f32)
    ones = same.astype(bf16)
    pick = (
        lax.broadcasted_iota(jnp.int32, (mini, both), 0)
        == lax.rem(lax.broadcasted_iota(jnp.int32, (mini, both), 1), mini)
    ).astype(f32)

    def per_row(pair):
        return jnp.concatenate(
            [
                jnp.broadcast_to(pair[:1], (mini, inner)),
                jnp.broadcast_to(pair[1:], (mini, inner)),
            ],
            axis=0,
        )

    def halves(x):
        low = lane_low(x.shape)
        first = jnp.sum(jnp.where(low, x, 0.0), axis=1, keepdims=True)
        second = jnp.sum(jnp.where(low, 0.0, x), axis=1, keepdims=True)
        return jnp.concatenate([first, second], axis=0)

    def spread(col):
        low = lane_low((mini, both))
        return jnp.where(low, col[:mini], col[mini:])

    def keys_of(j, m):
        return kv_s[j, m, pl.ds(0, mini), :]

    def step(j, m, state, z1, kb, key_cat, nxt, query):
        w1, b1, w2, b2 = state
        w1h, w2h = w1.astype(bf16), w2.astype(bf16)
        value_cat = kv_s[j, m, pl.ds(mini, mini), :].astype(f32)
        rate_rows = kv_s[j, m, pl.ds(both, PACK), :].astype(f32)
        e = halves(pick * (rate_rows[:1] + rate_rows[1:2]))
        u = gain * (bias - (value_cat - key_cat.astype(f32)))
        u_mean = halves(u) * (1.0 / d)

        x2h, slope = gelu_both(z1)
        x2h = x2h.astype(bf16)
        z = lane_cat(dot(x2h, w2h)) + b2
        scaled = gain_sq * z
        rs = lax.rsqrt(halves(z * z) * (1.0 / d) + ln_eps)
        mean_g = rs * halves(scaled) * (1.0 / d) + u_mean
        mean_gn = rs * (rs * halves(scaled * z) + halves(u * z)) * (1.0 / d)
        alpha = e * rs
        pulled = dot(blocks(u), w2h, NT)
        back = dot(jnp.concatenate([blocks(scaled), blocks(z)], axis=0), w2h, NT)
        d1 = (alpha * rs) * (back[:both] - mean_gn * back[both:]) + alpha * pulled
        h1h = (d1 * slope).astype(bf16)
        h1 = h1h.astype(f32)
        h2 = spread(alpha) * ((gain_sq - spread(mean_gn)) * (spread(rs) * z) + (u - spread(mean_g)))
        h2h = blocks(h2).astype(bf16)

        z1_next, kb_next, result = None, None, None
        streams = [] if nxt is None else [blocks(nxt)]
        if query is not None:
            streams.append(blocks(query))
        streams = jnp.concatenate(streams, axis=0)
        against_keys = dot(streams, kb, NT)
        against_state = dot(streams, w1h)
        lhs = []
        if nxt is not None:
            kb_next = streams[:both]
            lhs += [(against_keys[:both] + same).astype(bf16)]
        if query is not None:
            lhs.append((causal * (against_keys[-both:] + 1.0)).astype(bf16))
        moved = dot(jnp.concatenate(lhs, axis=0), h1h)
        if nxt is not None:
            z1_next = against_state[:both] + per_row(b1) - moved[:both]
        if query is not None:
            first_bar = against_state[-both:] + per_row(b1) - moved[-both:]
            hidden_bar = gelu(first_bar).astype(bf16)
            attend_hidden = causal * (dot(hidden_bar, x2h, NT) + 1.0)
            zb = lane_cat(dot(hidden_bar, w2h) - dot(attend_hidden, h2h)) + b2
            var = spread(halves(zb * zb)) * (1.0 / d)
            result = query.astype(f32) + gain * (zb * lax.rsqrt(var + ln_eps)) + bias
            if nxt is None:
                return None, None, None, result

        w1 = w1 - dot(kb, h1h, TN)
        b1 = b1 - jnp.concatenate(
            [
                jnp.sum(h1[:mini], axis=0, keepdims=True),
                jnp.sum(h1[mini:], axis=0, keepdims=True),
            ],
            axis=0,
        )
        w2 = w2 - dot(x2h, h2h, TN)
        b2 = b2 - jnp.sum(h2, axis=0, keepdims=True)
        return (w1, b1, w2, b2), z1_next, kb_next, result

    for p in range(minis):
        at = pl.ds((p % (minis - 1)) * mini, mini)
        q_s[p ^ flip] = q_early[at, :] if p + 1 < minis else q_late[...]
    for j in range(seq_count):
        for p in range(minis):
            kv_s[j, p ^ flip] = kv_ref[j, pl.ds(p * (both + PACK), both + PACK), :]

    w2, b2 = w2_ref[0], b2_ref[...]
    w2 = w2 - jnp.mean(w2, axis=0, keepdims=True)
    b2 = b2 - jnp.mean(b2, axis=1, keepdims=True)
    w1_s[...] = jnp.concatenate([w1_ref[0], w1_ref[0]], axis=0)
    b1_s[...] = jnp.concatenate([b1_ref[...], b1_ref[...]], axis=0)
    w2_s[...] = jnp.concatenate([w2, w2], axis=0).T
    b2_s[...] = jnp.concatenate([b2, b2], axis=1)
    z1_s[...] = dot(blocks(keys_of(0, 0)), w1_s[...]) + per_row(b1_s[...])

    def segment(j, queries):
        state, z1 = (w1_s[...], b1_s[...], w2_s[...], b2_s[...]), z1_s[...]
        key_cat = keys_of(j, 0)
        kb = blocks(key_cat)
        for m in range(minis):
            if m + 1 < minis:
                nxt = keys_of(j, m + 1)
            else:
                nxt = None if queries else keys_of(j + 1, 0)
            query = q_s[m] if queries else None
            state, z1, kb, result = step(j, m, state, z1, kb, key_cat, nxt, query)
            if queries:
                out_ref[pl.ds(m * mini, mini), :] = result.astype(bf16)
            key_cat = nxt
        if not queries:
            w1_s[...], b1_s[...], w2_s[...], b2_s[...] = state
            z1_s[...] = z1

    def body(j, carry):
        segment(j, False)
        return carry

    lax.fori_loop(0, place, body, 0)
    segment(place, True)


def out_kernel(count, ids_ref, heads_ref, *refs):
    w_refs, out_ref = refs[:count], refs[count]
    _, rows, both = heads_ref.shape
    d = both // 2
    low = lane_low((rows, both))
    firsts, seconds = [], []
    per = heads_ref.shape[0] // count
    me = 2 * ids_ref[1] + ids_ref[2]
    order = [(me ^ i) * per + j for i in range(count) for j in range(per)]
    for h in range(0, len(order), 2):
        even, odd = heads_ref[order[h]].astype(f32), heads_ref[order[h + 1]].astype(f32)
        firsts.append(jnp.where(low, even, pltpu.roll(odd, d, 1)))
        seconds.append(jnp.where(low, pltpu.roll(even, d, 1), odd))
    lhs = jnp.concatenate(
        [jnp.concatenate(firsts, axis=1), jnp.concatenate(seconds, axis=1)], axis=0
    )
    weights = jnp.concatenate([w_ref[...] for w_ref in w_refs], axis=0)
    prod = dot(lhs, weights).astype(bf16)
    out_ref[0] = prod[:rows]
    out_ref[1] = prod[rows:]


def swapped(array, flip, senders=None):
    senders = range(lax.axis_size("row")) if senders is None else senders
    return lax.ppermute(array, "row", [(i, i ^ flip) for i in senders])


VMEM_LIMIT = 14 * 1024 * 1024


def on_device(
    tokens,
    w_qkv,
    w_rate,
    rate_bias,
    w_out,
    w_first_init,
    b_first_init,
    w_second_init,
    b_second_init,
    ln_gain,
    ln_bias,
):
    videos, tok_part, width = tokens.shape
    d = w_qkv.shape[0] // 3
    both = 2 * d
    row_count, seq_count = lax.axis_size("row"), lax.axis_size("seq")
    minis = tok_part * row_count // MINI
    paired = row_count == 8 and minis == 4
    vmem = pl.BlockSpec(memory_space=pltpu.VMEM)
    smem = pl.BlockSpec(memory_space=pltpu.SMEM)
    params = pltpu.CompilerParams(vmem_limit_bytes=VMEM_LIMIT)
    row = lax.axis_index("row") if paired else 0
    ids = jnp.stack([lax.axis_index("seq"), row // 2, row % 2]).astype(jnp.int32)
    bias = rate_bias.reshape(1, 1)

    def project(count, pieces, first, parts, weights, *before):
        rows = count * MINI
        total = count if first else minis
        out_shape = [
            jax.ShapeDtypeStruct((total * (2 * MINI + PACK), both), bf16),
            jax.ShapeDtypeStruct((rows, both), bf16),
        ]
        if first:
            out_shape.append(jax.ShapeDtypeStruct((4 * d, width), bf16))
        return pl.pallas_call(
            partial(project_kernel, count, pieces, first),
            out_shape=out_shape,
            in_specs=[smem] + [vmem] * (len(parts) + len(weights) + 1 + len(before)),
            out_specs=[vmem] * len(out_shape),
            scratch_shapes=[pltpu.VMEM((2 * rows, 4 * d), f32)],
            compiler_params=params,
            cost_estimate=pl.CostEstimate(
                flops=16 * rows * d * width, bytes_accessed=4_000_000, transcendentals=0
            ),
            name="project" if first else "finish",
        )(ids, *parts, *weights, bias, *before)

    if paired:
        far, near, own, w_own = lax.optimization_barrier(
            (swapped(tokens, 4), swapped(tokens, 2), swapped(tokens, 1), swapped(w_out, 1))
        )
        last = swapped(far, 2)
        w_early, _ = lax.optimization_barrier((w_out, far))
        w_mid = swapped(w_early, 6, (2, 3, 4, 5))
        early = [tokens, own, near, swapped(near, 1), far, swapped(far, 1)]
        kv_early, q_early, stack = project(3, 2, True, early, (w_qkv, w_rate))
        last, kv_early, w_mid = lax.optimization_barrier((last, kv_early, w_mid))
        late = [last, swapped(last, 1)]
        w_after, _ = lax.optimization_barrier((w_out, last))
        w_parts = [w_out, swapped(w_after, 2), swapped(w_after, 4), swapped(w_after, 6, (0, 1, 6, 7))]
        kv, q_late = project(1, 2, False, late, (stack,), kv_early)
    else:
        whole = lax.all_gather(tokens, "row", axis=1, tiled=True)
        whole = whole.reshape(videos, minis, MINI, width)
        parts = [whole[:, m] for m in range(minis)]
        kv_early, q_early, stack = project(minis - 1, 1, True, parts[:-1], (w_qkv, w_rate))
        kv, q_late = project(1, 1, False, parts[-1:], (stack,), kv_early)
        w_parts = [lax.all_gather(w_out, "row", axis=0, tiled=True)]

    inner = w_first_init.shape[2]
    operands = [lax.all_gather(kv, "seq"), q_early, q_late, ln_gain, ln_bias]
    operands += [w_first_init, b_first_init]
    operands += [jnp.swapaxes(w_second_init, 1, 2), b_second_init]
    heads = pl.pallas_call(
        partial(chain_kernel, seq_count),
        out_shape=jax.ShapeDtypeStruct((minis * MINI, both), bf16),
        in_specs=[smem] + [vmem] * len(operands),
        out_specs=vmem,
        scratch_shapes=[
            pltpu.VMEM((seq_count, minis, 2 * MINI + PACK, both), bf16),
            pltpu.VMEM((minis, MINI, both), bf16),
            pltpu.VMEM((both, inner), f32),
            pltpu.VMEM((2, inner), f32),
            pltpu.VMEM((inner, both), f32),
            pltpu.VMEM((1, both), f32),
            pltpu.VMEM((2 * MINI, inner), f32),
        ],
        compiler_params=params,
        name="chain",
    )(ids, *operands)
    if paired:
        w_parts = list(lax.optimization_barrier((heads, *w_parts))[1:])
        w_parts[3] = w_parts[3] + w_mid
        w_parts = [w_parts[0], w_own] + [x for w in w_parts[1:] for x in (w, swapped(w, 1))]
    heads = heads.reshape(row_count, tok_part, both)
    arrived = lax.all_to_all(heads, "row", split_axis=0, concat_axis=0, tiled=True)
    return pl.pallas_call(
        partial(out_kernel, len(w_parts)),
        out_shape=jax.ShapeDtypeStruct((videos, tok_part, width), bf16),
        in_specs=[smem, vmem] + [vmem] * len(w_parts),
        out_specs=vmem,
        compiler_params=params,
        name="mix",
    )(ids, arrived, *w_parts)


def solution(mesh):
    in_specs = (
        P(None, ("seq", "row"), None),
        P("row", None),
        P("row", None),
        P("row"),
        P("row", None),
        P("row", None, None),
        P("row", None),
        P("row", None, None),
        P("row", None),
        P("row", None),
        P("row", None),
    )
    out_specs = P(None, ("seq", "row"), None)
    return jax.shard_map(
        on_device, mesh=mesh, in_specs=in_specs, out_specs=out_specs, check_vma=False
    )
```

```python
from functools import partial

import jax
import jax.numpy as jnp
from jax import lax
from jax.experimental import pallas as pl
from jax.experimental.pallas import tpu as pltpu
from jax.sharding import PartitionSpec as P

MINI = 64
gelu_coef = 0.7978845608028654
gelu_cubic = 0.044715
base_rate = 0.01
ln_eps = 1e-06

f32 = jnp.float32
bf16 = jnp.bfloat16
NN = ((1,), (0,))
NT = ((1,), (1,))
TN = ((0,), (0,))


def dot(left, right, dims=NN):
    return lax.dot_general(
        left.astype(bf16), right.astype(bf16), (dims, ((), ())), preferred_element_type=f32
    )


def lane_low(shape):
    return lax.broadcasted_iota(jnp.int32, shape, len(shape) - 1) < shape[-1] // 2


def blocks(cat):
    low = lane_low(cat.shape)
    zero = jnp.zeros_like(cat)
    return jnp.concatenate([jnp.where(low, cat, zero), jnp.where(low, zero, cat)], axis=0)


def lane_cat(rows):
    half = rows.shape[0] // 2
    return jnp.where(lane_low((half, rows.shape[1])), rows[:half], rows[half:])


PACK = 16


def project_kernel(count, pieces, first, ids_ref, *refs):
    x_refs, refs = refs[: count * pieces], refs[count * pieces :]
    if first:
        w_ref, wr_ref, bias_ref, kv_ref, q_ref, stack_ref, prod_s = refs
        d, base = w_ref.shape[0] // 3, 0
        stack_ref[: 3 * d, :] = w_ref[...]
        stack_ref[3 * d :, :] = jnp.broadcast_to(wr_ref[...], (d, wr_ref.shape[1]))
    else:
        stack_ref, bias_ref, early_ref, kv_ref, q_ref, prod_s = refs
        d = stack_ref.shape[0] // 4
        base = early_ref.shape[0]
        kv_ref[:base, :] = early_ref[...]
    mini = d
    both = 2 * mini
    part = x_refs[0].shape[1]
    x = jnp.concatenate([x_ref[...].reshape(-1, x_ref.shape[2]) for x_ref in x_refs], axis=0)
    prod = dot(x, stack_ref[...], NT)
    core = ids_ref[2]
    for i in range(count):
        for j in range(pieces):
            where = (core if j == 0 else 1 - core) * part if pieces > 1 else 0
            for video in range(2):
                row = ((i * pieces + j) * 2 + video) * part
                spot = i * both + video * mini + where
                if pieces > 1:
                    spot = pl.multiple_of(spot, part)
                prod_s[pl.ds(spot, part), :] = prod[row : row + part]
    eye = (
        lax.broadcasted_iota(jnp.int32, (both, both), 0)
        == lax.broadcasted_iota(jnp.int32, (both, both), 1)
    ).astype(f32)
    low = lane_low((mini, 2 * d))
    for i in range(count):
        prod = prod_s[pl.ds(i * both, both), :]
        qk, vr = prod[:, : 2 * d], prod[:, 2 * d :]
        qk_swap, vr_swap = pltpu.roll(qk, d, 1), pltpu.roll(vr, d, 1)
        keys = jnp.where(low, qk_swap[:mini], qk[mini:])
        queries = jnp.where(low, qk[:mini], qk_swap[mini:])
        values = jnp.where(low, vr[:mini], vr_swap[mini:])
        logits = jnp.where(lane_low(vr.shape), vr_swap, vr)
        logits = jnp.sum(logits * eye, axis=0, keepdims=True)
        rate = base_rate * jax.nn.sigmoid(logits + bias_ref[...]) / mini
        high = rate.astype(bf16).astype(f32)
        pad = jnp.zeros((PACK - 2, both), f32)
        at = base + i * (both + PACK)
        kv_ref[pl.ds(at, mini), :] = keys.astype(bf16)
        kv_ref[pl.ds(at + mini, mini), :] = values.astype(bf16)
        kv_ref[pl.ds(at + both, PACK), :] = jnp.concatenate([high, rate - high, pad], axis=0).astype(bf16)
        q_ref[pl.ds(i * mini, mini), :] = queries.astype(bf16)


def gelu_both(z):
    square = z * z
    tangent = jnp.tanh(z * (gelu_coef + (gelu_coef * gelu_cubic) * square))
    half = 0.5 * z
    value = half + half * tangent
    slope = (0.5 + 0.5 * tangent) + (half - half * (tangent * tangent)) * (
        gelu_coef + (3.0 * gelu_coef * gelu_cubic) * square
    )
    return value, slope


def gelu(z):
    tangent = jnp.tanh(z * (gelu_coef + (gelu_coef * gelu_cubic) * (z * z)))
    half = 0.5 * z
    return half + half * tangent


def chain_kernel(seq_count, ids_ref, *refs):
    kv_ref, refs = refs[0], refs[1:]
    q_early, q_late, gain_ref, bias_ref, w1_ref, b1_ref, w2_ref, b2_ref = refs[:8]
    out_ref, kv_s, q_s, w1_s, b1_s, w2_s, b2_s, z1_s = refs[8:]
    inner = w1_ref.shape[-1]
    both = gain_ref.shape[1] * 2
    d = both // 2
    mini = d
    minis = kv_s.shape[1]
    place, flip = ids_ref[0], ids_ref[1]
    gain = jnp.concatenate([gain_ref[...], gain_ref[...]], axis=1)
    bias = jnp.concatenate([bias_ref[...], bias_ref[...]], axis=1)
    gain_sq = gain * gain
    row_id = lax.broadcasted_iota(jnp.int32, (both, both), 0)
    lane_id = lax.broadcasted_iota(jnp.int32, (both, both), 1)
    same = ((row_id < mini) == (lane_id < mini)).astype(f32)
    causal = same * (row_id >= lane_id).astype(f32)
    ones = same.astype(bf16)
    pick = (
        lax.broadcasted_iota(jnp.int32, (mini, both), 0)
        == lax.rem(lax.broadcasted_iota(jnp.int32, (mini, both), 1), mini)
    ).astype(f32)

    def per_row(pair):
        return jnp.concatenate(
            [
                jnp.broadcast_to(pair[:1], (mini, inner)),
                jnp.broadcast_to(pair[1:], (mini, inner)),
            ],
            axis=0,
        )

    def halves(x):
        low = lane_low(x.shape)
        first = jnp.sum(jnp.where(low, x, 0.0), axis=1, keepdims=True)
        second = jnp.sum(jnp.where(low, 0.0, x), axis=1, keepdims=True)
        return jnp.concatenate([first, second], axis=0)

    def spread(col):
        low = lane_low((mini, both))
        return jnp.where(low, col[:mini], col[mini:])

    def keys_of(j, m):
        return kv_s[j, m, pl.ds(0, mini), :]

    def step(j, m, state, z1, kb, key_cat, nxt, query):
        w1, b1, w2, b2 = state
        w1h, w2h = w1.astype(bf16), w2.astype(bf16)
        value_cat = kv_s[j, m, pl.ds(mini, mini), :].astype(f32)
        rate_rows = kv_s[j, m, pl.ds(both, PACK), :].astype(f32)
        e = halves(pick * (rate_rows[:1] + rate_rows[1:2]))
        u = gain * (bias - (value_cat - key_cat.astype(f32)))
        u_mean = halves(u) * (1.0 / d)

        x2h, slope = gelu_both(z1)
        x2h = x2h.astype(bf16)
        z = lane_cat(dot(x2h, w2h)) + b2
        scaled = gain_sq * z
        rs = lax.rsqrt(halves(z * z) * (1.0 / d) + ln_eps)
        mean_g = rs * halves(scaled) * (1.0 / d) + u_mean
        mean_gn = rs * (rs * halves(scaled * z) + halves(u * z)) * (1.0 / d)
        alpha = e * rs
        pulled = dot(blocks(u), w2h, NT)
        back = dot(jnp.concatenate([blocks(scaled), blocks(z)], axis=0), w2h, NT)
        d1 = (alpha * rs) * (back[:both] - mean_gn * back[both:]) + alpha * pulled
        h1h = (d1 * slope).astype(bf16)
        h1 = h1h.astype(f32)
        h2 = spread(alpha) * ((gain_sq - spread(mean_gn)) * (spread(rs) * z) + (u - spread(mean_g)))
        h2h = blocks(h2).astype(bf16)

        z1_next, kb_next, result = None, None, None
        streams = [] if nxt is None else [blocks(nxt)]
        if query is not None:
            streams.append(blocks(query))
        streams = jnp.concatenate(streams, axis=0)
        against_keys = dot(streams, kb, NT)
        against_state = dot(streams, w1h)
        lhs = []
        if nxt is not None:
            kb_next = streams[:both]
            lhs += [(against_keys[:both] + same).astype(bf16)]
        if query is not None:
            lhs.append((causal * (against_keys[-both:] + 1.0)).astype(bf16))
        moved = dot(jnp.concatenate(lhs, axis=0), h1h)
        if nxt is not None:
            z1_next = against_state[:both] + per_row(b1) - moved[:both]
        if query is not None:
            first_bar = against_state[-both:] + per_row(b1) - moved[-both:]
            hidden_bar = gelu(first_bar).astype(bf16)
            attend_hidden = causal * (dot(hidden_bar, x2h, NT) + 1.0)
            zb = lane_cat(dot(hidden_bar, w2h) - dot(attend_hidden, h2h)) + b2
            var = spread(halves(zb * zb)) * (1.0 / d)
            result = query.astype(f32) + gain * (zb * lax.rsqrt(var + ln_eps)) + bias
            if nxt is None:
                return None, None, None, result

        w1 = w1 - dot(kb, h1h, TN)
        b1 = b1 - jnp.concatenate(
            [
                jnp.sum(h1[:mini], axis=0, keepdims=True),
                jnp.sum(h1[mini:], axis=0, keepdims=True),
            ],
            axis=0,
        )
        w2 = w2 - dot(x2h, h2h, TN)
        b2 = b2 - jnp.sum(h2, axis=0, keepdims=True)
        return (w1, b1, w2, b2), z1_next, kb_next, result

    for p in range(minis):
        at = pl.ds((p % (minis - 1)) * mini, mini)
        q_s[p ^ flip] = q_early[at, :] if p + 1 < minis else q_late[...]
    for j in range(seq_count):
        for p in range(minis):
            kv_s[j, p ^ flip] = kv_ref[j, pl.ds(p * (both + PACK), both + PACK), :]

    w2, b2 = w2_ref[0], b2_ref[...]
    w2 = w2 - jnp.mean(w2, axis=0, keepdims=True)
    b2 = b2 - jnp.mean(b2, axis=1, keepdims=True)
    w1_s[...] = jnp.concatenate([w1_ref[0], w1_ref[0]], axis=0)
    b1_s[...] = jnp.concatenate([b1_ref[...], b1_ref[...]], axis=0)
    w2_s[...] = jnp.concatenate([w2, w2], axis=0).T
    b2_s[...] = jnp.concatenate([b2, b2], axis=1)
    z1_s[...] = dot(blocks(keys_of(0, 0)), w1_s[...]) + per_row(b1_s[...])

    def segment(j, queries):
        state, z1 = (w1_s[...], b1_s[...], w2_s[...], b2_s[...]), z1_s[...]
        key_cat = keys_of(j, 0)
        kb = blocks(key_cat)
        for m in range(minis):
            if m + 1 < minis:
                nxt = keys_of(j, m + 1)
            else:
                nxt = None if queries else keys_of(j + 1, 0)
            query = q_s[m] if queries else None
            state, z1, kb, result = step(j, m, state, z1, kb, key_cat, nxt, query)
            if queries:
                out_ref[pl.ds(m * mini, mini), :] = result.astype(bf16)
            key_cat = nxt
        if not queries:
            w1_s[...], b1_s[...], w2_s[...], b2_s[...] = state
            z1_s[...] = z1

    def body(j, carry):
        segment(j, False)
        return carry

    lax.fori_loop(0, place, body, 0)
    segment(place, True)


def out_kernel(count, ids_ref, heads_ref, *refs):
    w_refs, refs = refs[:count], refs[count:]
    out_ref = refs[0]
    heads, rows, both = heads_ref.shape
    d = both // 2
    low = lane_low((rows, both))
    me = 2 * ids_ref[1] + ids_ref[2]
    order = list(range(heads)) if count == 1 else [me ^ i for i in range(heads)]
    firsts, seconds = [], []
    for h in range(0, heads, 2):
        even, odd = heads_ref[order[h]].astype(f32), heads_ref[order[h + 1]].astype(f32)
        firsts.append(jnp.where(low, even, pltpu.roll(odd, d, 1)))
        seconds.append(jnp.where(low, pltpu.roll(even, d, 1), odd))
    lhs = jnp.concatenate(
        [jnp.concatenate(firsts, axis=1), jnp.concatenate(seconds, axis=1)], axis=0
    )
    weights = [w_ref[...] for w_ref in w_refs]
    if count > 1:
        w_s = refs[1]
        share = d // 4
        for i in range(2):
            for flip in range(4):
                at = pl.multiple_of(i * d + (ids_ref[0] ^ flip) * share, share)
                w_s[pl.ds(at, share), :] = w_refs[count - 2 + i][pl.ds(flip * share, share), :]
        weights = weights[:-2] + [w_s[...]]
    prod = dot(lhs, jnp.concatenate(weights, axis=0)).astype(bf16)
    out_ref[0] = prod[:rows]
    out_ref[1] = prod[rows:]


def swapped(array, flip, axis="row"):
    return lax.ppermute(array, axis, [(i, i ^ flip) for i in range(lax.axis_size(axis))])


VMEM_LIMIT = 14 * 1024 * 1024


def on_device(
    tokens,
    w_qkv,
    w_rate,
    rate_bias,
    w_out,
    w_first_init,
    b_first_init,
    w_second_init,
    b_second_init,
    ln_gain,
    ln_bias,
):
    videos, tok_part, width = tokens.shape
    d = w_qkv.shape[0] // 3
    both = 2 * d
    row_count, seq_count = lax.axis_size("row"), lax.axis_size("seq")
    minis = tok_part * row_count // MINI
    paired = row_count == 8 and minis == 4 and seq_count == 4 and d == 64
    vmem = pl.BlockSpec(memory_space=pltpu.VMEM)
    smem = pl.BlockSpec(memory_space=pltpu.SMEM)
    params = pltpu.CompilerParams(vmem_limit_bytes=VMEM_LIMIT)
    row = lax.axis_index("row") if paired else 0
    ids = jnp.stack([lax.axis_index("seq"), row // 2, row % 2]).astype(jnp.int32)
    bias = rate_bias.reshape(1, 1)

    def project(count, pieces, first, parts, weights, *before):
        rows = count * MINI
        total = count if first else minis
        out_shape = [
            jax.ShapeDtypeStruct((total * (2 * MINI + PACK), both), bf16),
            jax.ShapeDtypeStruct((rows, both), bf16),
        ]
        if first:
            out_shape.append(jax.ShapeDtypeStruct((4 * d, width), bf16))
        return pl.pallas_call(
            partial(project_kernel, count, pieces, first),
            out_shape=out_shape,
            in_specs=[smem] + [vmem] * (len(parts) + len(weights) + 1 + len(before)),
            out_specs=[vmem] * len(out_shape),
            scratch_shapes=[pltpu.VMEM((2 * rows, 4 * d), f32)],
            compiler_params=params,
            cost_estimate=pl.CostEstimate(
                flops=16 * rows * d * width, bytes_accessed=4_000_000, transcendentals=0
            ),
            name="project" if first else "finish",
        )(ids, *parts, *weights, bias, *before)

    if paired:
        share = w_out.shape[0] // seq_count
        place = lax.axis_index("seq")
        far, near = swapped(tokens, 4), swapped(tokens, 2)
        own, w_own = swapped(tokens, 1), swapped(w_out, 1)
        w_share = swapped(lax.dynamic_slice_in_dim(w_out, place * share, share, 0), 6)
        w_end = [w_share] + [swapped(w_share, flip, "seq") for flip in range(1, seq_count)]
        w_end = jnp.concatenate(w_end, axis=0)
        w_end_other = swapped(w_end, 1)
        far, near, own, w_own, w_end, w_end_other = lax.optimization_barrier(
            (far, near, own, w_own, w_end, w_end_other)
        )
        last = swapped(far, 2)
        early = [tokens, own, near, swapped(near, 1), far, swapped(far, 1)]
        kv_early, q_early, stack = project(3, 2, True, early, (w_qkv, w_rate))
        last, kv_early = lax.optimization_barrier((last, kv_early))
        late = [last, swapped(last, 1)]
        w_after, _ = lax.optimization_barrier((w_out, last))
        w_far, w_near = swapped(w_after, 4), swapped(w_after, 2)
        kv, q_late = project(1, 2, False, late, (stack,), kv_early)
    else:
        whole = lax.all_gather(tokens, "row", axis=1, tiled=True)
        whole = whole.reshape(videos, minis, MINI, width)
        parts = [whole[:, m] for m in range(minis)]
        kv_early, q_early, stack = project(minis - 1, 1, True, parts[:-1], (w_qkv, w_rate))
        kv, q_late = project(1, 1, False, parts[-1:], (stack,), kv_early)
        w_parts = [lax.all_gather(w_out, "row", axis=0, tiled=True)]

    inner = w_first_init.shape[2]
    operands = [lax.all_gather(kv, "seq"), q_early, q_late, ln_gain, ln_bias]
    operands += [w_first_init, b_first_init]
    operands += [jnp.swapaxes(w_second_init, 1, 2), b_second_init]
    heads = pl.pallas_call(
        partial(chain_kernel, seq_count),
        out_shape=jax.ShapeDtypeStruct((minis * MINI, both), bf16),
        in_specs=[smem] + [vmem] * len(operands),
        out_specs=vmem,
        scratch_shapes=[
            pltpu.VMEM((seq_count, minis, 2 * MINI + PACK, both), bf16),
            pltpu.VMEM((minis, MINI, both), bf16),
            pltpu.VMEM((both, inner), f32),
            pltpu.VMEM((2, inner), f32),
            pltpu.VMEM((inner, both), f32),
            pltpu.VMEM((1, both), f32),
            pltpu.VMEM((2 * MINI, inner), f32),
        ],
        compiler_params=params,
        name="chain",
    )(ids, *operands)
    if paired:
        w_far, w_near, _ = lax.optimization_barrier((w_far, w_near, heads))
        w_parts = [w_out, w_own, w_near, swapped(w_near, 1), w_far, swapped(w_far, 1)]
        w_parts += [w_end, w_end_other]
    heads = heads.reshape(row_count, tok_part, both)
    arrived = lax.all_to_all(heads, "row", split_axis=0, concat_axis=0, tiled=True)
    return pl.pallas_call(
        partial(out_kernel, len(w_parts)),
        out_shape=jax.ShapeDtypeStruct((videos, tok_part, width), bf16),
        in_specs=[smem, vmem] + [vmem] * len(w_parts),
        out_specs=vmem,
        scratch_shapes=[pltpu.VMEM((2 * d, width), bf16)] if paired else [],
        compiler_params=params,
        name="mix",
    )(ids, arrived, *w_parts)


def solution(mesh):
    in_specs = (
        P(None, ("seq", "row"), None),
        P("row", None),
        P("row", None),
        P("row"),
        P("row", None),
        P("row", None, None),
        P("row", None),
        P("row", None, None),
        P("row", None),
        P("row", None),
        P("row", None),
    )
    out_specs = P(None, ("seq", "row"), None)
    return jax.shard_map(
        on_device, mesh=mesh, in_specs=in_specs, out_specs=out_specs, check_vma=False
    )
```

```python
from functools import partial

import jax
import jax.numpy as jnp
from jax import lax
from jax.experimental import pallas as pl
from jax.experimental.pallas import tpu as pltpu
from jax.sharding import PartitionSpec as P

MINI = 64
gelu_coef = 0.7978845608028654
gelu_cubic = 0.044715
base_rate = 0.01
ln_eps = 1e-06

f32 = jnp.float32
bf16 = jnp.bfloat16
NN = ((1,), (0,))
NT = ((1,), (1,))
TN = ((0,), (0,))


def dot(left, right, dims=NN):
    return lax.dot_general(
        left.astype(bf16), right.astype(bf16), (dims, ((), ())), preferred_element_type=f32
    )


def lane_low(shape):
    return lax.broadcasted_iota(jnp.int32, shape, len(shape) - 1) < shape[-1] // 2


def blocks(cat):
    low = lane_low(cat.shape)
    zero = jnp.zeros_like(cat)
    return jnp.concatenate([jnp.where(low, cat, zero), jnp.where(low, zero, cat)], axis=0)


def lane_cat(rows):
    half = rows.shape[0] // 2
    return jnp.where(lane_low((half, rows.shape[1])), rows[:half], rows[half:])


PACK = 16


def project_kernel(count, pieces, first, ids_ref, *refs):
    x_refs, refs = refs[: count * pieces], refs[count * pieces :]
    if first:
        w_ref, wr_ref, bias_ref, kv_ref, q_ref, stack_ref, prod_s = refs
        d, base = w_ref.shape[0] // 3, 0
        stack_ref[: 3 * d, :] = w_ref[...]
        stack_ref[3 * d :, :] = jnp.broadcast_to(wr_ref[...], (d, wr_ref.shape[1]))
    else:
        stack_ref, bias_ref, early_ref, kv_ref, q_ref, prod_s = refs
        d = stack_ref.shape[0] // 4
        base = early_ref.shape[0]
        kv_ref[:base, :] = early_ref[...]
    mini = d
    both = 2 * mini
    part = x_refs[0].shape[1]
    x = jnp.concatenate([x_ref[...].reshape(-1, x_ref.shape[2]) for x_ref in x_refs], axis=0)
    prod = dot(x, stack_ref[...], NT)
    core = ids_ref[2]
    for i in range(count):
        for j in range(pieces):
            where = (core if j == 0 else 1 - core) * part if pieces > 1 else 0
            for video in range(2):
                row = ((i * pieces + j) * 2 + video) * part
                spot = i * both + video * mini + where
                if pieces > 1:
                    spot = pl.multiple_of(spot, part)
                prod_s[pl.ds(spot, part), :] = prod[row : row + part]
    eye = (
        lax.broadcasted_iota(jnp.int32, (both, both), 0)
        == lax.broadcasted_iota(jnp.int32, (both, both), 1)
    ).astype(f32)
    low = lane_low((mini, 2 * d))
    for i in range(count):
        prod = prod_s[pl.ds(i * both, both), :]
        qk, vr = prod[:, : 2 * d], prod[:, 2 * d :]
        qk_swap, vr_swap = pltpu.roll(qk, d, 1), pltpu.roll(vr, d, 1)
        keys = jnp.where(low, qk_swap[:mini], qk[mini:])
        queries = jnp.where(low, qk[:mini], qk_swap[mini:])
        values = jnp.where(low, vr[:mini], vr_swap[mini:])
        logits = jnp.where(lane_low(vr.shape), vr_swap, vr)
        logits = jnp.sum(logits * eye, axis=0, keepdims=True)
        rate = base_rate * jax.nn.sigmoid(logits + bias_ref[...]) / mini
        high = rate.astype(bf16).astype(f32)
        pad = jnp.zeros((PACK - 2, both), f32)
        at = base + i * (both + PACK)
        kv_ref[pl.ds(at, mini), :] = keys.astype(bf16)
        kv_ref[pl.ds(at + mini, mini), :] = values.astype(bf16)
        kv_ref[pl.ds(at + both, PACK), :] = jnp.concatenate([high, rate - high, pad], axis=0).astype(bf16)
        q_ref[pl.ds(i * mini, mini), :] = queries.astype(bf16)


def gelu_both(z):
    square = z * z
    tangent = jnp.tanh(z * (gelu_coef + (gelu_coef * gelu_cubic) * square))
    half = 0.5 * z
    value = half + half * tangent
    slope = (0.5 + 0.5 * tangent) + (half - half * (tangent * tangent)) * (
        gelu_coef + (3.0 * gelu_coef * gelu_cubic) * square
    )
    return value, slope


def gelu(z):
    tangent = jnp.tanh(z * (gelu_coef + (gelu_coef * gelu_cubic) * (z * z)))
    half = 0.5 * z
    return half + half * tangent


def chain_kernel(seq_count, ids_ref, *refs):
    kv_ref, refs = refs[0], refs[1:]
    q_early, q_late, gain_ref, bias_ref, w1_ref, b1_ref, w2_ref, b2_ref = refs[:8]
    out_ref, kv_s, q_s, w1_s, b1_s, w2_s, b2_s, z1_s = refs[8:]
    inner = w1_ref.shape[-1]
    both = gain_ref.shape[1] * 2
    d = both // 2
    mini = d
    minis = kv_s.shape[1]
    place, flip = ids_ref[0], ids_ref[1]
    gain = jnp.concatenate([gain_ref[...], gain_ref[...]], axis=1)
    bias = jnp.concatenate([bias_ref[...], bias_ref[...]], axis=1)
    gain_sq = gain * gain
    row_id = lax.broadcasted_iota(jnp.int32, (both, both), 0)
    lane_id = lax.broadcasted_iota(jnp.int32, (both, both), 1)
    same = ((row_id < mini) == (lane_id < mini)).astype(f32)
    causal = same * (row_id >= lane_id).astype(f32)
    ones = same.astype(bf16)
    pick = (
        lax.broadcasted_iota(jnp.int32, (mini, both), 0)
        == lax.rem(lax.broadcasted_iota(jnp.int32, (mini, both), 1), mini)
    ).astype(f32)

    def per_row(pair):
        return jnp.concatenate(
            [
                jnp.broadcast_to(pair[:1], (mini, inner)),
                jnp.broadcast_to(pair[1:], (mini, inner)),
            ],
            axis=0,
        )

    def halves(x):
        low = lane_low(x.shape)
        first = jnp.sum(jnp.where(low, x, 0.0), axis=1, keepdims=True)
        second = jnp.sum(jnp.where(low, 0.0, x), axis=1, keepdims=True)
        return jnp.concatenate([first, second], axis=0)

    def spread(col):
        low = lane_low((mini, both))
        return jnp.where(low, col[:mini], col[mini:])

    def keys_of(j, m):
        return kv_s[j, m, pl.ds(0, mini), :]

    def step(j, m, state, z1, kb, key_cat, nxt, query):
        w1, b1, w2, b2 = state
        w1h, w2h = w1.astype(bf16), w2.astype(bf16)
        value_cat = kv_s[j, m, pl.ds(mini, mini), :].astype(f32)
        rate_rows = kv_s[j, m, pl.ds(both, PACK), :].astype(f32)
        e = halves(pick * (rate_rows[:1] + rate_rows[1:2]))
        u = gain * (bias - (value_cat - key_cat.astype(f32)))
        u_mean = halves(u) * (1.0 / d)

        x2h, slope = gelu_both(z1)
        x2h = x2h.astype(bf16)
        z = lane_cat(dot(x2h, w2h)) + b2
        scaled = gain_sq * z
        rs = lax.rsqrt(halves(z * z) * (1.0 / d) + ln_eps)
        mean_g = rs * halves(scaled) * (1.0 / d) + u_mean
        mean_gn = rs * (rs * halves(scaled * z) + halves(u * z)) * (1.0 / d)
        alpha = e * rs
        pulled = dot(blocks(u), w2h, NT)
        back = dot(jnp.concatenate([blocks(scaled), blocks(z)], axis=0), w2h, NT)
        d1 = (alpha * rs) * (back[:both] - mean_gn * back[both:]) + alpha * pulled
        h1h = (d1 * slope).astype(bf16)
        h1 = h1h.astype(f32)
        h2 = spread(alpha) * ((gain_sq - spread(mean_gn)) * (spread(rs) * z) + (u - spread(mean_g)))
        h2h = blocks(h2).astype(bf16)

        z1_next, kb_next, result = None, None, None
        streams = [] if nxt is None else [blocks(nxt)]
        if query is not None:
            streams.append(blocks(query))
        streams = jnp.concatenate(streams, axis=0)
        against_keys = dot(streams, kb, NT)
        against_state = dot(streams, w1h)
        lhs = []
        if nxt is not None:
            kb_next = streams[:both]
            lhs += [(against_keys[:both] + same).astype(bf16)]
        if query is not None:
            lhs.append((causal * (against_keys[-both:] + 1.0)).astype(bf16))
        moved = dot(jnp.concatenate(lhs, axis=0), h1h)
        if nxt is not None:
            z1_next = against_state[:both] + per_row(b1) - moved[:both]
        if query is not None:
            first_bar = against_state[-both:] + per_row(b1) - moved[-both:]
            hidden_bar = gelu(first_bar).astype(bf16)
            attend_hidden = causal * (dot(hidden_bar, x2h, NT) + 1.0)
            zb = lane_cat(dot(hidden_bar, w2h) - dot(attend_hidden, h2h)) + b2
            var = spread(halves(zb * zb)) * (1.0 / d)
            result = query.astype(f32) + gain * (zb * lax.rsqrt(var + ln_eps)) + bias
            if nxt is None:
                return None, None, None, result

        w1 = w1 - dot(kb, h1h, TN)
        b1 = b1 - jnp.concatenate(
            [
                jnp.sum(h1[:mini], axis=0, keepdims=True),
                jnp.sum(h1[mini:], axis=0, keepdims=True),
            ],
            axis=0,
        )
        w2 = w2 - dot(x2h, h2h, TN)
        b2 = b2 - jnp.sum(h2, axis=0, keepdims=True)
        return (w1, b1, w2, b2), z1_next, kb_next, result

    for p in range(minis):
        at = pl.ds((p % (minis - 1)) * mini, mini)
        q_s[p ^ flip] = q_early[at, :] if p + 1 < minis else q_late[...]
    for j in range(seq_count):
        for p in range(minis):
            kv_s[j, p ^ flip] = kv_ref[j, pl.ds(p * (both + PACK), both + PACK), :]

    w2, b2 = w2_ref[0], b2_ref[...]
    w2 = w2 - jnp.mean(w2, axis=0, keepdims=True)
    b2 = b2 - jnp.mean(b2, axis=1, keepdims=True)
    w1_s[...] = jnp.concatenate([w1_ref[0], w1_ref[0]], axis=0)
    b1_s[...] = jnp.concatenate([b1_ref[...], b1_ref[...]], axis=0)
    w2_s[...] = jnp.concatenate([w2, w2], axis=0).T
    b2_s[...] = jnp.concatenate([b2, b2], axis=1)
    z1_s[...] = dot(blocks(keys_of(0, 0)), w1_s[...]) + per_row(b1_s[...])

    def segment(j, queries):
        state, z1 = (w1_s[...], b1_s[...], w2_s[...], b2_s[...]), z1_s[...]
        key_cat = keys_of(j, 0)
        kb = blocks(key_cat)
        for m in range(minis):
            if m + 1 < minis:
                nxt = keys_of(j, m + 1)
            else:
                nxt = None if queries else keys_of(j + 1, 0)
            query = q_s[m] if queries else None
            state, z1, kb, result = step(j, m, state, z1, kb, key_cat, nxt, query)
            if queries:
                out_ref[pl.ds(m * mini, mini), :] = result.astype(bf16)
            key_cat = nxt
        if not queries:
            w1_s[...], b1_s[...], w2_s[...], b2_s[...] = state
            z1_s[...] = z1

    def body(j, carry):
        segment(j, False)
        return carry

    lax.fori_loop(0, place, body, 0)
    segment(place, True)


def out_kernel(count, ids_ref, heads_ref, *refs):
    w_refs, out_ref, w_s = refs[:count], refs[count], refs[-1]
    heads, rows, both = heads_ref.shape
    d = both // 2
    low = lane_low((rows, both))
    me = 2 * ids_ref[1] + ids_ref[2]
    order = list(range(heads)) if count == 1 else [me ^ i for i in range(heads)]
    firsts, seconds = [], []
    for h in range(0, heads, 2):
        even, odd = heads_ref[order[h]].astype(f32), heads_ref[order[h + 1]].astype(f32)
        firsts.append(jnp.where(low, even, pltpu.roll(odd, d, 1)))
        seconds.append(jnp.where(low, pltpu.roll(even, d, 1), odd))
    lhs = jnp.concatenate(
        [jnp.concatenate(firsts, axis=1), jnp.concatenate(seconds, axis=1)], axis=0
    )
    weights = [w_ref[...] for w_ref in w_refs]
    if count > 1:
        share = d // 4
        for i in range(2):
            for flip in range(4):
                at = pl.multiple_of(i * d + (ids_ref[0] ^ flip) * share, share)
                w_s[pl.ds(at, share), :] = w_refs[count - 2 + i][pl.ds(flip * share, share), :]
        weights = weights[:-2] + [w_s[...]]
    prod = dot(lhs, jnp.concatenate(weights, axis=0)).astype(bf16)
    out_ref[0] = prod[:rows]
    out_ref[1] = prod[rows:]


def swapped(array, flip, axis="row"):
    return lax.ppermute(array, axis, [(i, i ^ flip) for i in range(lax.axis_size(axis))])


VMEM_LIMIT = 14 * 1024 * 1024


def on_device(
    tokens,
    w_qkv,
    w_rate,
    rate_bias,
    w_out,
    w_first_init,
    b_first_init,
    w_second_init,
    b_second_init,
    ln_gain,
    ln_bias,
):
    videos, tok_part, width = tokens.shape
    d = w_qkv.shape[0] // 3
    both = 2 * d
    row_count, seq_count = lax.axis_size("row"), lax.axis_size("seq")
    minis = tok_part * row_count // MINI
    paired = row_count == 8 and minis == 4 and seq_count == 4
    vmem = pl.BlockSpec(memory_space=pltpu.VMEM)
    smem = pl.BlockSpec(memory_space=pltpu.SMEM)
    params = pltpu.CompilerParams(vmem_limit_bytes=VMEM_LIMIT)
    row = lax.axis_index("row") if paired else 0
    ids = jnp.stack([lax.axis_index("seq"), row // 2, row % 2]).astype(jnp.int32)
    bias = rate_bias.reshape(1, 1)

    def project(count, pieces, first, parts, weights, *before):
        rows = count * MINI
        total = count if first else minis
        out_shape = [
            jax.ShapeDtypeStruct((total * (2 * MINI + PACK), both), bf16),
            jax.ShapeDtypeStruct((rows, both), bf16),
        ]
        if first:
            out_shape.append(jax.ShapeDtypeStruct((4 * d, width), bf16))
        return pl.pallas_call(
            partial(project_kernel, count, pieces, first),
            out_shape=out_shape,
            in_specs=[smem] + [vmem] * (len(parts) + len(weights) + 1 + len(before)),
            out_specs=[vmem] * len(out_shape),
            scratch_shapes=[pltpu.VMEM((2 * rows, 4 * d), f32)],
            compiler_params=params,
            cost_estimate=pl.CostEstimate(
                flops=16 * rows * d * width, bytes_accessed=4_000_000, transcendentals=0
            ),
            name="project" if first else "finish",
        )(ids, *parts, *weights, bias, *before)

    if paired:
        share = w_out.shape[0] // seq_count
        place = lax.axis_index("seq")
        far, near = swapped(tokens, 4), swapped(tokens, 2)
        own, w_own = swapped(tokens, 1), swapped(w_out, 1)
        w_share = lax.dynamic_slice_in_dim(w_out, place * share, share, 0)
        w_share = swapped(w_share, 6)
        far, near, own, w_own, w_share = lax.optimization_barrier((far, near, own, w_own, w_share))
        last = swapped(far, 2)
        near_other, far_other = swapped(near, 1), swapped(far, 1)
        w_end = [w_share] + [swapped(w_share, flip, "seq") for flip in range(1, seq_count)]
        early = [tokens, own, near, near_other, far, far_other]
        kv_early, q_early, stack = project(3, 2, True, early, (w_qkv, w_rate))
        last, kv_early, *w_end = lax.optimization_barrier((last, kv_early, *w_end))
        w_end = jnp.concatenate(w_end, axis=0)
        late = [last, swapped(last, 1)]
        w_after, _ = lax.optimization_barrier((w_out, last))
        w_far, w_near = swapped(w_after, 4), swapped(w_after, 2)
        kv, q_late = project(1, 2, False, late, (stack,), kv_early)
    else:
        whole = lax.all_gather(tokens, "row", axis=1, tiled=True)
        whole = whole.reshape(videos, minis, MINI, width)
        parts = [whole[:, m] for m in range(minis)]
        kv_early, q_early, stack = project(minis - 1, 1, True, parts[:-1], (w_qkv, w_rate))
        kv, q_late = project(1, 1, False, parts[-1:], (stack,), kv_early)
        w_parts = [lax.all_gather(w_out, "row", axis=0, tiled=True)]

    inner = w_first_init.shape[2]
    operands = [lax.all_gather(kv, "seq"), q_early, q_late, ln_gain, ln_bias]
    operands += [w_first_init, b_first_init]
    operands += [jnp.swapaxes(w_second_init, 1, 2), b_second_init]
    heads = pl.pallas_call(
        partial(chain_kernel, seq_count),
        out_shape=jax.ShapeDtypeStruct((minis * MINI, both), bf16),
        in_specs=[smem] + [vmem] * len(operands),
        out_specs=vmem,
        scratch_shapes=[
            pltpu.VMEM((seq_count, minis, 2 * MINI + PACK, both), bf16),
            pltpu.VMEM((minis, MINI, both), bf16),
            pltpu.VMEM((both, inner), f32),
            pltpu.VMEM((2, inner), f32),
            pltpu.VMEM((inner, both), f32),
            pltpu.VMEM((1, both), f32),
            pltpu.VMEM((2 * MINI, inner), f32),
        ],
        compiler_params=params,
        name="chain",
    )(ids, *operands)
    if paired:
        w_near, w_far, w_end, _ = lax.optimization_barrier((w_near, w_far, w_end, heads))
        w_parts = [w_out, w_own] + [x for w in (w_near, w_far, w_end) for x in (w, swapped(w, 1))]
    heads = heads.reshape(row_count, tok_part, both)
    arrived = lax.all_to_all(heads, "row", split_axis=0, concat_axis=0, tiled=True)
    return pl.pallas_call(
        partial(out_kernel, len(w_parts)),
        out_shape=jax.ShapeDtypeStruct((videos, tok_part, width), bf16),
        in_specs=[smem, vmem] + [vmem] * len(w_parts),
        out_specs=vmem,
        scratch_shapes=[pltpu.VMEM((2 * d, width), bf16)],
        compiler_params=params,
        name="mix",
    )(ids, arrived, *w_parts)


def solution(mesh):
    in_specs = (
        P(None, ("seq", "row"), None),
        P("row", None),
        P("row", None),
        P("row"),
        P("row", None),
        P("row", None, None),
        P("row", None),
        P("row", None, None),
        P("row", None),
        P("row", None),
        P("row", None),
    )
    out_specs = P(None, ("seq", "row"), None)
    return jax.shard_map(
        on_device, mesh=mesh, in_specs=in_specs, out_specs=out_specs, check_vma=False
    )
```

```python
from functools import partial

import jax
import jax.numpy as jnp
from jax import lax
from jax.experimental import pallas as pl
from jax.experimental.pallas import tpu as pltpu
from jax.sharding import PartitionSpec as P

MINI = 64
gelu_coef = 0.7978845608028654
gelu_cubic = 0.044715
base_rate = 0.01
ln_eps = 1e-06

f32 = jnp.float32
bf16 = jnp.bfloat16
NN = ((1,), (0,))
NT = ((1,), (1,))
TN = ((0,), (0,))


def dot(left, right, dims=NN):
    return lax.dot_general(
        left.astype(bf16), right.astype(bf16), (dims, ((), ())), preferred_element_type=f32
    )


def halved(x):
    high = x.astype(bf16)
    return high, (x - high.astype(f32)).astype(bf16)


def lane_low(shape):
    return lax.broadcasted_iota(jnp.int32, shape, len(shape) - 1) < shape[-1] // 2


def blocks(cat):
    low = lane_low(cat.shape)
    zero = jnp.zeros_like(cat)
    return jnp.concatenate([jnp.where(low, cat, zero), jnp.where(low, zero, cat)], axis=0)


def lane_cat(rows):
    half = rows.shape[0] // 2
    return jnp.where(lane_low((half, rows.shape[1])), rows[:half], rows[half:])


PACK = 16
MIX_CHUNKS = 4


def project_kernel(count, pieces, first, ids_ref, *refs):
    x_refs, refs = refs[: count * pieces], refs[count * pieces :]
    if first:
        w_ref, wr_ref, bias_ref, kv_ref, q_ref, stack_ref, prod_s = refs
        d, base = w_ref.shape[0] // 3, 0
        stack_ref[: 3 * d, :] = w_ref[...]
        stack_ref[3 * d :, :] = jnp.broadcast_to(wr_ref[...], (d, wr_ref.shape[1]))
    else:
        stack_ref, bias_ref, early_ref, kv_ref, q_ref, prod_s = refs
        d = stack_ref.shape[0] // 4
        base = early_ref.shape[0]
        kv_ref[:base, :] = early_ref[...]
    mini = d
    both = 2 * mini
    part = x_refs[0].shape[1]
    x = jnp.concatenate([x_ref[...].reshape(-1, x_ref.shape[2]) for x_ref in x_refs], axis=0)
    prod = dot(x, stack_ref[...], NT)
    core = ids_ref[2]
    for i in range(count):
        for j in range(pieces):
            where = (core if j == 0 else 1 - core) * part if pieces > 1 else 0
            for video in range(2):
                row = ((i * pieces + j) * 2 + video) * part
                spot = i * both + video * mini + where
                if pieces > 1:
                    spot = pl.multiple_of(spot, part)
                prod_s[pl.ds(spot, part), :] = prod[row : row + part]
    eye = (
        lax.broadcasted_iota(jnp.int32, (both, both), 0)
        == lax.broadcasted_iota(jnp.int32, (both, both), 1)
    ).astype(f32)
    low = lane_low((mini, 2 * d))
    for i in range(count):
        prod = prod_s[pl.ds(i * both, both), :]
        qk, vr = prod[:, : 2 * d], prod[:, 2 * d :]
        qk_swap, vr_swap = pltpu.roll(qk, d, 1), pltpu.roll(vr, d, 1)
        keys = jnp.where(low, qk_swap[:mini], qk[mini:])
        queries = jnp.where(low, qk[:mini], qk_swap[mini:])
        values = jnp.where(low, vr[:mini], vr_swap[mini:])
        logits = jnp.where(lane_low(vr.shape), vr_swap, vr)
        logits = jnp.sum(logits * eye, axis=0, keepdims=True)
        rate = base_rate * jax.nn.sigmoid(logits + bias_ref[...]) / mini
        high = rate.astype(bf16).astype(f32)
        pad = jnp.zeros((PACK - 2, both), f32)
        at = base + i * (both + PACK)
        kv_ref[pl.ds(at, mini), :] = keys.astype(bf16)
        kv_ref[pl.ds(at + mini, mini), :] = values.astype(bf16)
        kv_ref[pl.ds(at + both, PACK), :] = jnp.concatenate([high, rate - high, pad], axis=0).astype(bf16)
        q_ref[pl.ds(i * mini, mini), :] = queries.astype(bf16)


def gelu_both(z):
    square = z * z
    tangent = jnp.tanh(z * (gelu_coef + (gelu_coef * gelu_cubic) * square))
    half = 0.5 * z
    value = half + half * tangent
    slope = (0.5 + 0.5 * tangent) + (half - half * (tangent * tangent)) * (
        gelu_coef + (3.0 * gelu_coef * gelu_cubic) * square
    )
    return value, slope


def gelu(z):
    tangent = jnp.tanh(z * (gelu_coef + (gelu_coef * gelu_cubic) * (z * z)))
    half = 0.5 * z
    return half + half * tangent


def chain_kernel(seq_count, ids_ref, *refs):
    kv_ref, refs = refs[0], refs[1:]
    q_early, q_late, gain_ref, bias_ref, w1_ref, b1_ref, w2_ref, b2_ref = refs[:8]
    out_ref, kv_s, q_s, w1_s, b1_s, w2_s, b2_s, z1_s = refs[8:]
    inner = w1_ref.shape[-1]
    both = gain_ref.shape[1] * 2
    d = both // 2
    mini = d
    minis = kv_s.shape[1]
    place, flip = ids_ref[0], ids_ref[1]
    gain = jnp.concatenate([gain_ref[...], gain_ref[...]], axis=1)
    bias = jnp.concatenate([bias_ref[...], bias_ref[...]], axis=1)
    gain_sq = gain * gain
    row_id = lax.broadcasted_iota(jnp.int32, (both, both), 0)
    lane_id = lax.broadcasted_iota(jnp.int32, (both, both), 1)
    same = ((row_id < mini) == (lane_id < mini)).astype(f32)
    causal = same * (row_id >= lane_id).astype(f32)
    ones = same.astype(bf16)
    pick = (
        lax.broadcasted_iota(jnp.int32, (mini, both), 0)
        == lax.rem(lax.broadcasted_iota(jnp.int32, (mini, both), 1), mini)
    ).astype(f32)

    def per_row(pair):
        return jnp.concatenate(
            [
                jnp.broadcast_to(pair[:1], (mini, inner)),
                jnp.broadcast_to(pair[1:], (mini, inner)),
            ],
            axis=0,
        )

    def halves(x):
        low = lane_low(x.shape)
        first = jnp.sum(jnp.where(low, x, 0.0), axis=1, keepdims=True)
        second = jnp.sum(jnp.where(low, 0.0, x), axis=1, keepdims=True)
        return jnp.concatenate([first, second], axis=0)

    def spread(col):
        low = lane_low((mini, both))
        return jnp.where(low, col[:mini], col[mini:])

    def keys_of(j, m):
        return kv_s[j, m, pl.ds(0, mini), :]

    def step(j, m, state, z1, kb, key_cat, nxt, query):
        w1, b1, w2, b2 = state
        w1h, (w2h, w2l) = w1.astype(bf16), halved(w2)
        value_cat = kv_s[j, m, pl.ds(mini, mini), :].astype(f32)
        rate_rows = kv_s[j, m, pl.ds(both, PACK), :].astype(f32)
        e = halves(pick * (rate_rows[:1] + rate_rows[1:2]))
        u = gain * (bias - (value_cat - key_cat.astype(f32)))
        u_mean = halves(u) * (1.0 / d)

        x2, slope = gelu_both(z1)
        x2h, x2l = halved(x2)
        pieces = dot(x2h, jnp.concatenate([w2h, w2l], axis=1))
        z = lane_cat(pieces[:, :both] + (pieces[:, both:] + dot(x2l, w2h))) + b2
        scaled = gain_sq * z
        rs = lax.rsqrt(halves(z * z) * (1.0 / d) + ln_eps)
        mean_g = rs * halves(scaled) * (1.0 / d) + u_mean
        mean_gn = rs * (rs * halves(scaled * z) + halves(u * z)) * (1.0 / d)
        alpha = e * rs
        pulled = dot(blocks(u), w2h, NT)
        back = dot(jnp.concatenate([blocks(scaled), blocks(z)], axis=0), w2h, NT)
        d1 = (alpha * rs) * (back[:both] - mean_gn * back[both:]) + alpha * pulled
        h1h = (d1 * slope).astype(bf16)
        h1 = h1h.astype(f32)
        h2 = spread(alpha) * ((gain_sq - spread(mean_gn)) * (spread(rs) * z) + (u - spread(mean_g)))
        h2h, h2l = (blocks(x) for x in halved(h2))

        z1_next, kb_next, result = None, None, None
        streams = [] if nxt is None else [blocks(nxt)]
        if query is not None:
            streams.append(blocks(query))
        streams = jnp.concatenate(streams, axis=0)
        against_keys = dot(streams, kb, NT)
        against_state = dot(streams, w1h)
        lhs = []
        if nxt is not None:
            kb_next = streams[:both]
            lhs += [(against_keys[:both] + same).astype(bf16)]
        if query is not None:
            lhs.append((causal * (against_keys[-both:] + 1.0)).astype(bf16))
        moved = dot(jnp.concatenate(lhs, axis=0), h1h)
        if nxt is not None:
            z1_next = against_state[:both] + per_row(b1) - moved[:both]
        if query is not None:
            first_bar = against_state[-both:] + per_row(b1) - moved[-both:]
            hidden_bar = gelu(first_bar).astype(bf16)
            attend_hidden = causal * (dot(hidden_bar, x2h, NT) + 1.0)
            zb = lane_cat(dot(hidden_bar, w2h) - dot(attend_hidden, h2h)) + b2
            var = spread(halves(zb * zb)) * (1.0 / d)
            result = query.astype(f32) + gain * (zb * lax.rsqrt(var + ln_eps)) + bias
            if nxt is None:
                return None, None, None, result

        w1 = w1 - dot(kb, h1h, TN)
        b1 = b1 - jnp.concatenate(
            [
                jnp.sum(h1[:mini], axis=0, keepdims=True),
                jnp.sum(h1[mini:], axis=0, keepdims=True),
            ],
            axis=0,
        )
        w2 = w2 - dot(
            jnp.concatenate([x2h, x2l, x2h], axis=0), jnp.concatenate([h2h, h2h, h2l], axis=0), TN
        )
        b2 = b2 - jnp.sum(h2, axis=0, keepdims=True)
        return (w1, b1, w2, b2), z1_next, kb_next, result

    for p in range(minis):
        at = pl.ds((p % (minis - 1)) * mini, mini)
        q_s[p ^ flip] = q_early[at, :] if p + 1 < minis else q_late[...]
    for j in range(seq_count):
        for p in range(minis):
            kv_s[j, p ^ flip] = kv_ref[j, pl.ds(p * (both + PACK), both + PACK), :]

    w2, b2 = w2_ref[0], b2_ref[...]
    w2 = w2 - jnp.mean(w2, axis=0, keepdims=True)
    b2 = b2 - jnp.mean(b2, axis=1, keepdims=True)
    w1_s[...] = jnp.concatenate([w1_ref[0], w1_ref[0]], axis=0)
    b1_s[...] = jnp.concatenate([b1_ref[...], b1_ref[...]], axis=0)
    w2_s[...] = jnp.concatenate([w2, w2], axis=0).T
    b2_s[...] = jnp.concatenate([b2, b2], axis=1)
    z1_s[...] = dot(blocks(keys_of(0, 0)), w1_s[...]) + per_row(b1_s[...])

    def segment(j, queries):
        state, z1 = (w1_s[...], b1_s[...], w2_s[...], b2_s[...]), z1_s[...]
        key_cat = keys_of(j, 0)
        kb = blocks(key_cat)
        for m in range(minis):
            if m + 1 < minis:
                nxt = keys_of(j, m + 1)
            else:
                nxt = None if queries else keys_of(j + 1, 0)
            query = q_s[m] if queries else None
            state, z1, kb, result = step(j, m, state, z1, kb, key_cat, nxt, query)
            if queries:
                out_ref[pl.ds(m * mini, mini), :] = result.astype(bf16)
            key_cat = nxt
        if not queries:
            w1_s[...], b1_s[...], w2_s[...], b2_s[...] = state
            z1_s[...] = z1

    def body(j, carry):
        segment(j, False)
        return carry

    lax.fori_loop(0, place, body, 0)
    segment(place, True)


def out_kernel(count, ids_ref, heads_ref, *refs):
    w_refs, (out_ref, w_s, out_s, sems) = refs[:count], refs[count:]
    heads, rows, both = heads_ref.shape
    d = both // 2
    low = lane_low((rows, both))
    me = 2 * ids_ref[1] + ids_ref[2]
    order = list(range(heads)) if count == 1 else [me ^ i for i in range(heads)]
    firsts, seconds = [], []
    for h in range(0, heads, 2):
        even, odd = heads_ref[order[h]].astype(f32), heads_ref[order[h + 1]].astype(f32)
        firsts.append(jnp.where(low, even, pltpu.roll(odd, d, 1)))
        seconds.append(jnp.where(low, pltpu.roll(even, d, 1), odd))
    lhs = jnp.concatenate(
        [jnp.concatenate(firsts, axis=1), jnp.concatenate(seconds, axis=1)], axis=0
    )
    share = d // 4
    for i in range(2 if count > 1 else 0):
        for flip in range(4):
            at = pl.multiple_of(i * d + (ids_ref[0] ^ flip) * share, share)
            w_s[pl.ds(at, share), :] = w_refs[count - 2 + i][pl.ds(flip * share, share), :]
    whole = w_refs if count == 1 else [*w_refs[:-2], w_s]
    cols = out_s.shape[3]
    copies = []
    for c in range(out_s.shape[0]):
        lanes = slice(c * cols, (c + 1) * cols)
        prod = dot(lhs, jnp.concatenate([w[:, lanes] for w in whole], axis=0)).astype(bf16)
        out_s[c, 0] = prod[:rows]
        out_s[c, 1] = prod[rows:]
        copies.append(pltpu.make_async_copy(out_s.at[c], out_ref.at[:, :, lanes], sems.at[c]))
        copies[-1].start()
    for copy in copies:
        copy.wait()


def swapped(array, flip, axis="row"):
    return lax.ppermute(array, axis, [(i, i ^ flip) for i in range(lax.axis_size(axis))])


VMEM_LIMIT = 14 * 1024 * 1024


def on_device(
    tokens,
    w_qkv,
    w_rate,
    rate_bias,
    w_out,
    w_first_init,
    b_first_init,
    w_second_init,
    b_second_init,
    ln_gain,
    ln_bias,
):
    videos, tok_part, width = tokens.shape
    d = w_qkv.shape[0] // 3
    both = 2 * d
    row_count, seq_count = lax.axis_size("row"), lax.axis_size("seq")
    minis = tok_part * row_count // MINI
    paired = row_count == 8 and minis == 4 and seq_count == 4
    vmem = pl.BlockSpec(memory_space=pltpu.VMEM)
    smem = pl.BlockSpec(memory_space=pltpu.SMEM)
    params = pltpu.CompilerParams(vmem_limit_bytes=VMEM_LIMIT)
    row = lax.axis_index("row") if paired else 0
    ids = jnp.stack([lax.axis_index("seq"), row // 2, row % 2]).astype(jnp.int32)
    bias = rate_bias.reshape(1, 1)

    def project(count, pieces, first, parts, weights, *before):
        rows = count * MINI
        total = count if first else minis
        out_shape = [
            jax.ShapeDtypeStruct((total * (2 * MINI + PACK), both), bf16),
            jax.ShapeDtypeStruct((rows, both), bf16),
        ]
        if first:
            out_shape.append(jax.ShapeDtypeStruct((4 * d, width), bf16))
        return pl.pallas_call(
            partial(project_kernel, count, pieces, first),
            out_shape=out_shape,
            in_specs=[smem] + [vmem] * (len(parts) + len(weights) + 1 + len(before)),
            out_specs=[vmem] * len(out_shape),
            scratch_shapes=[pltpu.VMEM((2 * rows, 4 * d), f32)],
            compiler_params=params,
            cost_estimate=pl.CostEstimate(
                flops=16 * rows * d * width, bytes_accessed=4_000_000, transcendentals=0
            ),
            name="project" if first else "finish",
        )(ids, *parts, *weights, bias, *before)

    if paired:
        share = w_out.shape[0] // seq_count
        place = lax.axis_index("seq")
        far, near = swapped(tokens, 4), swapped(tokens, 2)
        own, w_own = swapped(tokens, 1), swapped(w_out, 1)
        w_share = lax.dynamic_slice_in_dim(w_out, place * share, share, 0)
        w_share = swapped(w_share, 6)
        far, near, own, w_own, w_share = lax.optimization_barrier((far, near, own, w_own, w_share))
        last = swapped(far, 2)
        near_other, far_other = swapped(near, 1), swapped(far, 1)
        w_end = [w_share] + [swapped(w_share, flip, "seq") for flip in range(1, seq_count)]
        early = [tokens, own, near, near_other, far, far_other]
        kv_early, q_early, stack = project(3, 2, True, early, (w_qkv, w_rate))
        last, kv_early, *w_end = lax.optimization_barrier((last, kv_early, *w_end))
        w_end = jnp.concatenate(w_end, axis=0)
        late = [last, swapped(last, 1)]
        w_after, _ = lax.optimization_barrier((w_out, last))
        w_far, w_near = swapped(w_after, 4), swapped(w_after, 2)
        kv, q_late = project(1, 2, False, late, (stack,), kv_early)
    else:
        whole = lax.all_gather(tokens, "row", axis=1, tiled=True)
        whole = whole.reshape(videos, minis, MINI, width)
        parts = [whole[:, m] for m in range(minis)]
        kv_early, q_early, stack = project(minis - 1, 1, True, parts[:-1], (w_qkv, w_rate))
        kv, q_late = project(1, 1, False, parts[-1:], (stack,), kv_early)
        w_parts = [lax.all_gather(w_out, "row", axis=0, tiled=True)]

    inner = w_first_init.shape[2]
    operands = [lax.all_gather(kv, "seq"), q_early, q_late, ln_gain, ln_bias]
    operands += [w_first_init, b_first_init]
    operands += [jnp.swapaxes(w_second_init, 1, 2), b_second_init]
    heads = pl.pallas_call(
        partial(chain_kernel, seq_count),
        out_shape=jax.ShapeDtypeStruct((minis * MINI, both), bf16),
        in_specs=[smem] + [vmem] * len(operands),
        out_specs=vmem,
        scratch_shapes=[
            pltpu.VMEM((seq_count, minis, 2 * MINI + PACK, both), bf16),
            pltpu.VMEM((minis, MINI, both), bf16),
            pltpu.VMEM((both, inner), f32),
            pltpu.VMEM((2, inner), f32),
            pltpu.VMEM((inner, both), f32),
            pltpu.VMEM((1, both), f32),
            pltpu.VMEM((2 * MINI, inner), f32),
        ],
        compiler_params=params,
        name="chain",
    )(ids, *operands)
    if paired:
        w_near, w_far, w_end, _ = lax.optimization_barrier((w_near, w_far, w_end, heads))
        w_parts = [w_out, w_own] + [x for w in (w_near, w_far, w_end) for x in (w, swapped(w, 1))]
    heads = heads.reshape(row_count, tok_part, both)
    arrived = lax.all_to_all(heads, "row", split_axis=0, concat_axis=0, tiled=True)
    return pl.pallas_call(
        partial(out_kernel, len(w_parts)),
        out_shape=jax.ShapeDtypeStruct((videos, tok_part, width), bf16),
        in_specs=[smem, vmem] + [vmem] * len(w_parts),
        out_specs=pl.BlockSpec(memory_space=pl.ANY),
        scratch_shapes=[
            pltpu.VMEM((2 * d, width), bf16),
            pltpu.VMEM((MIX_CHUNKS, videos, tok_part, width // MIX_CHUNKS), bf16),
            pltpu.SemaphoreType.DMA((MIX_CHUNKS,)),
        ],
        compiler_params=params,
        name="mix",
    )(ids, arrived, *w_parts)


def solution(mesh):
    in_specs = (
        P(None, ("seq", "row"), None),
        P("row", None),
        P("row", None),
        P("row"),
        P("row", None),
        P("row", None, None),
        P("row", None),
        P("row", None, None),
        P("row", None),
        P("row", None),
        P("row", None),
    )
    out_specs = P(None, ("seq", "row"), None)
    return jax.shard_map(
        on_device, mesh=mesh, in_specs=in_specs, out_specs=out_specs, check_vma=False
    )
```

```python
from functools import partial

import jax
import jax.numpy as jnp
from jax import lax
from jax.experimental import pallas as pl
from jax.experimental.pallas import tpu as pltpu
from jax.sharding import PartitionSpec as P

MINI = 64
gelu_coef = 0.7978845608028654
gelu_cubic = 0.044715
base_rate = 0.01
ln_eps = 1e-06

f32 = jnp.float32
bf16 = jnp.bfloat16
NN = ((1,), (0,))
NT = ((1,), (1,))
TN = ((0,), (0,))


def dot(left, right, dims=NN):
    return lax.dot_general(
        left.astype(bf16), right.astype(bf16), (dims, ((), ())), preferred_element_type=f32
    )


def halved(x):
    high = x.astype(bf16)
    return high, (x - high.astype(f32)).astype(bf16)


def thirds(x):
    high = x.astype(bf16)
    rest = x - high.astype(f32)
    middle = rest.astype(bf16)
    return high, middle, (rest - middle.astype(f32)).astype(bf16)


def lane_low(shape):
    return lax.broadcasted_iota(jnp.int32, shape, len(shape) - 1) < shape[-1] // 2


def blocks(cat):
    low = lane_low(cat.shape)
    zero = jnp.zeros_like(cat)
    return jnp.concatenate([jnp.where(low, cat, zero), jnp.where(low, zero, cat)], axis=0)


def lane_cat(rows):
    half = rows.shape[0] // 2
    return jnp.where(lane_low((half, rows.shape[1])), rows[:half], rows[half:])


PACK = 16
MIX_CHUNKS = 4


def project_kernel(count, pieces, first, ids_ref, *refs):
    x_refs, refs = refs[: count * pieces], refs[count * pieces :]
    if first:
        w_ref, wr_ref, bias_ref, kv_ref, q_ref, stack_ref, prod_s = refs
        d, base = w_ref.shape[0] // 3, 0
        stack_ref[: 3 * d, :] = w_ref[...]
        stack_ref[3 * d :, :] = jnp.broadcast_to(wr_ref[...], (d, wr_ref.shape[1]))
    else:
        stack_ref, bias_ref, early_ref, kv_ref, q_ref, prod_s = refs
        d = stack_ref.shape[0] // 4
        base = early_ref.shape[0]
        kv_ref[:base, :] = early_ref[...]
    mini = d
    both = 2 * mini
    part = x_refs[0].shape[1]
    x = jnp.concatenate([x_ref[...].reshape(-1, x_ref.shape[2]) for x_ref in x_refs], axis=0)
    prod = dot(x, stack_ref[...], NT)
    core = ids_ref[2]
    for i in range(count):
        for j in range(pieces):
            where = (core if j == 0 else 1 - core) * part if pieces > 1 else 0
            for video in range(2):
                row = ((i * pieces + j) * 2 + video) * part
                spot = i * both + video * mini + where
                if pieces > 1:
                    spot = pl.multiple_of(spot, part)
                prod_s[pl.ds(spot, part), :] = prod[row : row + part]
    eye = (
        lax.broadcasted_iota(jnp.int32, (both, both), 0)
        == lax.broadcasted_iota(jnp.int32, (both, both), 1)
    ).astype(f32)
    low = lane_low((mini, 2 * d))
    for i in range(count):
        prod = prod_s[pl.ds(i * both, both), :]
        qk, vr = prod[:, : 2 * d], prod[:, 2 * d :]
        qk_swap, vr_swap = pltpu.roll(qk, d, 1), pltpu.roll(vr, d, 1)
        keys = jnp.where(low, qk_swap[:mini], qk[mini:])
        queries = jnp.where(low, qk[:mini], qk_swap[mini:])
        values = jnp.where(low, vr[:mini], vr_swap[mini:])
        logits = jnp.where(lane_low(vr.shape), vr_swap, vr)
        logits = jnp.sum(logits * eye, axis=0, keepdims=True)
        rate = base_rate * jax.nn.sigmoid(logits + bias_ref[...]) / mini
        high = rate.astype(bf16).astype(f32)
        pad = jnp.zeros((PACK - 2, both), f32)
        at = base + i * (both + PACK)
        kv_ref[pl.ds(at, mini), :] = keys.astype(bf16)
        kv_ref[pl.ds(at + mini, mini), :] = values.astype(bf16)
        kv_ref[pl.ds(at + both, PACK), :] = jnp.concatenate([high, rate - high, pad], axis=0).astype(bf16)
        q_ref[pl.ds(i * mini, mini), :] = queries.astype(bf16)


def gelu_both(z):
    square = z * z
    tangent = jnp.tanh(z * (gelu_coef + (gelu_coef * gelu_cubic) * square))
    half = 0.5 * z
    value = half + half * tangent
    slope = (0.5 + 0.5 * tangent) + (half - half * (tangent * tangent)) * (
        gelu_coef + (3.0 * gelu_coef * gelu_cubic) * square
    )
    return value, slope


def gelu(z):
    tangent = jnp.tanh(z * (gelu_coef + (gelu_coef * gelu_cubic) * (z * z)))
    half = 0.5 * z
    return half + half * tangent


def chain_kernel(seq_count, ids_ref, *refs):
    kv_ref, refs = refs[0], refs[1:]
    q_early, q_late, gain_ref, bias_ref, w1_ref, b1_ref, w2_ref, b2_ref = refs[:8]
    out_ref, kv_s, q_s, w1_s, b1_s, w2_s, b2_s, z1_s = refs[8:]
    inner = w1_ref.shape[-1]
    both = gain_ref.shape[1] * 2
    d = both // 2
    mini = d
    minis = kv_s.shape[1]
    place, flip = ids_ref[0], ids_ref[1]
    gain = jnp.concatenate([gain_ref[...], gain_ref[...]], axis=1)
    bias = jnp.concatenate([bias_ref[...], bias_ref[...]], axis=1)
    gain_sq = gain * gain
    row_id = lax.broadcasted_iota(jnp.int32, (both, both), 0)
    lane_id = lax.broadcasted_iota(jnp.int32, (both, both), 1)
    same = ((row_id < mini) == (lane_id < mini)).astype(f32)
    causal = same * (row_id >= lane_id).astype(f32)
    ones = same.astype(bf16)
    pick = (
        lax.broadcasted_iota(jnp.int32, (mini, both), 0)
        == lax.rem(lax.broadcasted_iota(jnp.int32, (mini, both), 1), mini)
    ).astype(f32)

    def per_row(pair):
        return jnp.concatenate(
            [
                jnp.broadcast_to(pair[:1], (mini, inner)),
                jnp.broadcast_to(pair[1:], (mini, inner)),
            ],
            axis=0,
        )

    def halves(x):
        low = lane_low(x.shape)
        first = jnp.sum(jnp.where(low, x, 0.0), axis=1, keepdims=True)
        second = jnp.sum(jnp.where(low, 0.0, x), axis=1, keepdims=True)
        return jnp.concatenate([first, second], axis=0)

    def spread(col):
        low = lane_low((mini, both))
        return jnp.where(low, col[:mini], col[mini:])

    def keys_of(j, m):
        return kv_s[j, m, pl.ds(0, mini), :]

    def step(j, m, state, z1, kb, key_cat, nxt, query):
        w1, b1, w2, b2 = state
        w1h, (w2h, w2m, w2l) = w1.astype(bf16), thirds(w2)
        value_cat = kv_s[j, m, pl.ds(mini, mini), :].astype(f32)
        rate_rows = kv_s[j, m, pl.ds(both, PACK), :].astype(f32)
        e = halves(pick * (rate_rows[:1] + rate_rows[1:2]))
        u = gain * (bias - (value_cat - key_cat.astype(f32)))
        u_mean = halves(u) * (1.0 / d)

        x2, slope = gelu_both(z1)
        x2h, x2m, x2l = thirds(x2)
        pieces = dot(
            jnp.concatenate([x2h, x2m, x2l], axis=0), jnp.concatenate([w2h, w2m], axis=1)
        )
        small = dot(x2h, w2l) + pieces[both : 2 * both, both:] + pieces[2 * both :, :both]
        medium = pieces[:both, both:] + pieces[both : 2 * both, :both]
        z = lane_cat(pieces[:both, :both] + (medium + small)) + b2
        scaled = gain_sq * z
        rs = lax.rsqrt(halves(z * z) * (1.0 / d) + ln_eps)
        mean_g = rs * halves(scaled) * (1.0 / d) + u_mean
        mean_gn = rs * (rs * halves(scaled * z) + halves(u * z)) * (1.0 / d)
        alpha = e * rs
        pulled = dot(blocks(u), w2h, NT)
        back = dot(jnp.concatenate([blocks(scaled), blocks(z)], axis=0), w2h, NT)
        d1 = (alpha * rs) * (back[:both] - mean_gn * back[both:]) + alpha * pulled
        h1h = (d1 * slope).astype(bf16)
        h1 = h1h.astype(f32)
        h2 = spread(alpha) * ((gain_sq - spread(mean_gn)) * (spread(rs) * z) + (u - spread(mean_g)))
        h2h, h2m, h2l = (blocks(x) for x in thirds(h2))

        z1_next, kb_next, result = None, None, None
        streams = [] if nxt is None else [blocks(nxt)]
        if query is not None:
            streams.append(blocks(query))
        streams = jnp.concatenate(streams, axis=0)
        against_keys = dot(streams, kb, NT)
        against_state = dot(streams, w1h)
        lhs = []
        if nxt is not None:
            kb_next = streams[:both]
            lhs += [(against_keys[:both] + same).astype(bf16)]
        if query is not None:
            lhs.append((causal * (against_keys[-both:] + 1.0)).astype(bf16))
        moved = dot(jnp.concatenate(lhs, axis=0), h1h)
        if nxt is not None:
            z1_next = against_state[:both] + per_row(b1) - moved[:both]
        if query is not None:
            first_bar = against_state[-both:] + per_row(b1) - moved[-both:]
            hidden_bar = gelu(first_bar).astype(bf16)
            attend_hidden = causal * (dot(hidden_bar, x2h, NT) + 1.0)
            zb = lane_cat(dot(hidden_bar, w2h) - dot(attend_hidden, h2h)) + b2
            var = spread(halves(zb * zb)) * (1.0 / d)
            result = query.astype(f32) + gain * (zb * lax.rsqrt(var + ln_eps)) + bias
            if nxt is None:
                return None, None, None, result

        w1 = w1 - dot(kb, h1h, TN)
        b1 = b1 - jnp.concatenate(
            [
                jnp.sum(h1[:mini], axis=0, keepdims=True),
                jnp.sum(h1[mini:], axis=0, keepdims=True),
            ],
            axis=0,
        )
        w2 = w2 - dot(
            jnp.concatenate([x2h, x2m, x2h, x2l, x2m, x2h], axis=0),
            jnp.concatenate([h2h, h2h, h2m, h2h, h2m, h2l], axis=0),
            TN,
        )
        b2 = b2 - jnp.sum(h2, axis=0, keepdims=True)
        return (w1, b1, w2, b2), z1_next, kb_next, result

    for p in range(minis):
        at = pl.ds((p % (minis - 1)) * mini, mini)
        q_s[p ^ flip] = q_early[at, :] if p + 1 < minis else q_late[...]
    for j in range(seq_count):
        for p in range(minis):
            kv_s[j, p ^ flip] = kv_ref[j, pl.ds(p * (both + PACK), both + PACK), :]

    w2, b2 = w2_ref[0], b2_ref[...]
    w2 = w2 - jnp.mean(w2, axis=0, keepdims=True)
    b2 = b2 - jnp.mean(b2, axis=1, keepdims=True)
    w1_s[...] = jnp.concatenate([w1_ref[0], w1_ref[0]], axis=0)
    b1_s[...] = jnp.concatenate([b1_ref[...], b1_ref[...]], axis=0)
    w2_s[...] = jnp.concatenate([w2, w2], axis=0).T
    b2_s[...] = jnp.concatenate([b2, b2], axis=1)
    z1_s[...] = dot(blocks(keys_of(0, 0)), w1_s[...]) + per_row(b1_s[...])

    def segment(j, queries):
        state, z1 = (w1_s[...], b1_s[...], w2_s[...], b2_s[...]), z1_s[...]
        key_cat = keys_of(j, 0)
        kb = blocks(key_cat)
        for m in range(minis):
            if m + 1 < minis:
                nxt = keys_of(j, m + 1)
            else:
                nxt = None if queries else keys_of(j + 1, 0)
            query = q_s[m] if queries else None
            state, z1, kb, result = step(j, m, state, z1, kb, key_cat, nxt, query)
            if queries:
                out_ref[pl.ds(m * mini, mini), :] = result.astype(bf16)
            key_cat = nxt
        if not queries:
            w1_s[...], b1_s[...], w2_s[...], b2_s[...] = state
            z1_s[...] = z1

    def body(j, carry):
        segment(j, False)
        return carry

    lax.fori_loop(0, place, body, 0)
    segment(place, True)


def out_kernel(count, ids_ref, heads_ref, *refs):
    w_refs, (out_ref, w_s, out_s, sems) = refs[:count], refs[count:]
    heads, rows, both = heads_ref.shape
    d = both // 2
    low = lane_low((rows, both))
    me = 2 * ids_ref[1] + ids_ref[2]
    order = list(range(heads)) if count == 1 else [me ^ i for i in range(heads)]
    firsts, seconds = [], []
    for h in range(0, heads, 2):
        even, odd = heads_ref[order[h]].astype(f32), heads_ref[order[h + 1]].astype(f32)
        firsts.append(jnp.where(low, even, pltpu.roll(odd, d, 1)))
        seconds.append(jnp.where(low, pltpu.roll(even, d, 1), odd))
    lhs = jnp.concatenate(
        [jnp.concatenate(firsts, axis=1), jnp.concatenate(seconds, axis=1)], axis=0
    )
    share = d // 4
    for i in range(2 if count > 1 else 0):
        for flip in range(4):
            at = pl.multiple_of(i * d + (ids_ref[0] ^ flip) * share, share)
            w_s[pl.ds(at, share), :] = w_refs[count - 2 + i][pl.ds(flip * share, share), :]
    whole = w_refs if count == 1 else [*w_refs[:-2], w_s]
    cols = out_s.shape[3]
    copies = []
    for c in range(out_s.shape[0]):
        lanes = slice(c * cols, (c + 1) * cols)
        prod = dot(lhs, jnp.concatenate([w[:, lanes] for w in whole], axis=0)).astype(bf16)
        out_s[c, 0] = prod[:rows]
        out_s[c, 1] = prod[rows:]
        copies.append(pltpu.make_async_copy(out_s.at[c], out_ref.at[:, :, lanes], sems.at[c]))
        copies[-1].start()
    for copy in copies:
        copy.wait()


def swapped(array, flip, axis="row"):
    return lax.ppermute(array, axis, [(i, i ^ flip) for i in range(lax.axis_size(axis))])


VMEM_LIMIT = 14 * 1024 * 1024


def on_device(
    tokens,
    w_qkv,
    w_rate,
    rate_bias,
    w_out,
    w_first_init,
    b_first_init,
    w_second_init,
    b_second_init,
    ln_gain,
    ln_bias,
):
    videos, tok_part, width = tokens.shape
    d = w_qkv.shape[0] // 3
    both = 2 * d
    row_count, seq_count = lax.axis_size("row"), lax.axis_size("seq")
    minis = tok_part * row_count // MINI
    paired = row_count == 8 and minis == 4 and seq_count == 4
    vmem = pl.BlockSpec(memory_space=pltpu.VMEM)
    smem = pl.BlockSpec(memory_space=pltpu.SMEM)
    params = pltpu.CompilerParams(vmem_limit_bytes=VMEM_LIMIT)
    row = lax.axis_index("row") if paired else 0
    ids = jnp.stack([lax.axis_index("seq"), row // 2, row % 2]).astype(jnp.int32)
    bias = rate_bias.reshape(1, 1)

    def project(count, pieces, first, parts, weights, *before):
        rows = count * MINI
        total = count if first else minis
        out_shape = [
            jax.ShapeDtypeStruct((total * (2 * MINI + PACK), both), bf16),
            jax.ShapeDtypeStruct((rows, both), bf16),
        ]
        if first:
            out_shape.append(jax.ShapeDtypeStruct((4 * d, width), bf16))
        return pl.pallas_call(
            partial(project_kernel, count, pieces, first),
            out_shape=out_shape,
            in_specs=[smem] + [vmem] * (len(parts) + len(weights) + 1 + len(before)),
            out_specs=[vmem] * len(out_shape),
            scratch_shapes=[pltpu.VMEM((2 * rows, 4 * d), f32)],
            compiler_params=params,
            cost_estimate=pl.CostEstimate(
                flops=16 * rows * d * width, bytes_accessed=4_000_000, transcendentals=0
            ),
            name="project" if first else "finish",
        )(ids, *parts, *weights, bias, *before)

    if paired:
        share = w_out.shape[0] // seq_count
        place = lax.axis_index("seq")
        far, near = swapped(tokens, 4), swapped(tokens, 2)
        own, w_own = swapped(tokens, 1), swapped(w_out, 1)
        w_share = lax.dynamic_slice_in_dim(w_out, place * share, share, 0)
        w_share = swapped(w_share, 6)
        far, near, own, w_own, w_share = lax.optimization_barrier((far, near, own, w_own, w_share))
        last = swapped(far, 2)
        near_other, far_other = swapped(near, 1), swapped(far, 1)
        w_end = [w_share] + [swapped(w_share, flip, "seq") for flip in range(1, seq_count)]
        early = [tokens, own, near, near_other, far, far_other]
        kv_early, q_early, stack = project(3, 2, True, early, (w_qkv, w_rate))
        last, kv_early, *w_end = lax.optimization_barrier((last, kv_early, *w_end))
        w_end = jnp.concatenate(w_end, axis=0)
        late = [last, swapped(last, 1)]
        w_after, _ = lax.optimization_barrier((w_out, last))
        w_far, w_near = swapped(w_after, 4), swapped(w_after, 2)
        kv, q_late = project(1, 2, False, late, (stack,), kv_early)
    else:
        whole = lax.all_gather(tokens, "row", axis=1, tiled=True)
        whole = whole.reshape(videos, minis, MINI, width)
        parts = [whole[:, m] for m in range(minis)]
        kv_early, q_early, stack = project(minis - 1, 1, True, parts[:-1], (w_qkv, w_rate))
        kv, q_late = project(1, 1, False, parts[-1:], (stack,), kv_early)
        w_parts = [lax.all_gather(w_out, "row", axis=0, tiled=True)]

    inner = w_first_init.shape[2]
    operands = [lax.all_gather(kv, "seq"), q_early, q_late, ln_gain, ln_bias]
    operands += [w_first_init, b_first_init]
    operands += [jnp.swapaxes(w_second_init, 1, 2), b_second_init]
    heads = pl.pallas_call(
        partial(chain_kernel, seq_count),
        out_shape=jax.ShapeDtypeStruct((minis * MINI, both), bf16),
        in_specs=[smem] + [vmem] * len(operands),
        out_specs=vmem,
        scratch_shapes=[
            pltpu.VMEM((seq_count, minis, 2 * MINI + PACK, both), bf16),
            pltpu.VMEM((minis, MINI, both), bf16),
            pltpu.VMEM((both, inner), f32),
            pltpu.VMEM((2, inner), f32),
            pltpu.VMEM((inner, both), f32),
            pltpu.VMEM((1, both), f32),
            pltpu.VMEM((2 * MINI, inner), f32),
        ],
        compiler_params=params,
        name="chain",
    )(ids, *operands)
    if paired:
        w_near, w_far, w_end, _ = lax.optimization_barrier((w_near, w_far, w_end, heads))
        w_parts = [w_out, w_own] + [x for w in (w_near, w_far, w_end) for x in (w, swapped(w, 1))]
    heads = heads.reshape(row_count, tok_part, both)
    arrived = lax.all_to_all(heads, "row", split_axis=0, concat_axis=0, tiled=True)
    return pl.pallas_call(
        partial(out_kernel, len(w_parts)),
        out_shape=jax.ShapeDtypeStruct((videos, tok_part, width), bf16),
        in_specs=[smem, vmem] + [vmem] * len(w_parts),
        out_specs=pl.BlockSpec(memory_space=pl.ANY),
        scratch_shapes=[
            pltpu.VMEM((2 * d, width), bf16),
            pltpu.VMEM((MIX_CHUNKS, videos, tok_part, width // MIX_CHUNKS), bf16),
            pltpu.SemaphoreType.DMA((MIX_CHUNKS,)),
        ],
        compiler_params=params,
        name="mix",
    )(ids, arrived, *w_parts)


def solution(mesh):
    in_specs = (
        P(None, ("seq", "row"), None),
        P("row", None),
        P("row", None),
        P("row"),
        P("row", None),
        P("row", None, None),
        P("row", None),
        P("row", None, None),
        P("row", None),
        P("row", None),
        P("row", None),
    )
    out_specs = P(None, ("seq", "row"), None)
    return jax.shard_map(
        on_device, mesh=mesh, in_specs=in_specs, out_specs=out_specs, check_vma=False
    )
```

```python
from functools import partial

import jax
import jax.numpy as jnp
from jax import lax
from jax.experimental import pallas as pl
from jax.experimental.pallas import tpu as pltpu
from jax.sharding import PartitionSpec as P

MINI = 64
gelu_coef = 0.7978845608028654
gelu_cubic = 0.044715
base_rate = 0.01
ln_eps = 1e-06

f32 = jnp.float32
bf16 = jnp.bfloat16
NN = ((1,), (0,))
NT = ((1,), (1,))
TN = ((0,), (0,))


def dot(left, right, dims=NN):
    return lax.dot_general(
        left.astype(bf16), right.astype(bf16), (dims, ((), ())), preferred_element_type=f32
    )


def halved(x):
    high = x.astype(bf16)
    return high, (x - high.astype(f32)).astype(bf16)


def thirds(x):
    high = x.astype(bf16)
    rest = x - high.astype(f32)
    middle = rest.astype(bf16)
    return high, middle, (rest - middle.astype(f32)).astype(bf16)


def lane_low(shape):
    return lax.broadcasted_iota(jnp.int32, shape, len(shape) - 1) < shape[-1] // 2


def blocks(cat):
    low = lane_low(cat.shape)
    zero = jnp.zeros_like(cat)
    return jnp.concatenate([jnp.where(low, cat, zero), jnp.where(low, zero, cat)], axis=0)


def lane_cat(rows):
    half = rows.shape[0] // 2
    return jnp.where(lane_low((half, rows.shape[1])), rows[:half], rows[half:])


PACK = 16
MIX_CHUNKS = 4


def project_kernel(count, pieces, first, ids_ref, *refs):
    x_refs, refs = refs[: count * pieces], refs[count * pieces :]
    if first:
        w_ref, wr_ref, bias_ref, kv_ref, q_ref, stack_ref, prod_s = refs
        d, base = w_ref.shape[0] // 3, 0
        stack_ref[: 3 * d, :] = w_ref[...]
        stack_ref[3 * d :, :] = jnp.broadcast_to(wr_ref[...], (d, wr_ref.shape[1]))
    else:
        stack_ref, bias_ref, early_ref, kv_ref, q_ref, prod_s = refs
        d = stack_ref.shape[0] // 4
        base = early_ref.shape[0]
        kv_ref[:base, :] = early_ref[...]
    mini = d
    both = 2 * mini
    part = x_refs[0].shape[1]
    x = jnp.concatenate([x_ref[...].reshape(-1, x_ref.shape[2]) for x_ref in x_refs], axis=0)
    prod = dot(x, stack_ref[...], NT)
    core = ids_ref[2]
    for i in range(count):
        for j in range(pieces):
            where = (core if j == 0 else 1 - core) * part if pieces > 1 else 0
            for video in range(2):
                row = ((i * pieces + j) * 2 + video) * part
                spot = i * both + video * mini + where
                if pieces > 1:
                    spot = pl.multiple_of(spot, part)
                prod_s[pl.ds(spot, part), :] = prod[row : row + part]
    eye = (
        lax.broadcasted_iota(jnp.int32, (both, both), 0)
        == lax.broadcasted_iota(jnp.int32, (both, both), 1)
    ).astype(f32)
    low = lane_low((mini, 2 * d))
    for i in range(count):
        prod = prod_s[pl.ds(i * both, both), :]
        qk, vr = prod[:, : 2 * d], prod[:, 2 * d :]
        qk_swap, vr_swap = pltpu.roll(qk, d, 1), pltpu.roll(vr, d, 1)
        keys = jnp.where(low, qk_swap[:mini], qk[mini:])
        queries = jnp.where(low, qk[:mini], qk_swap[mini:])
        values = jnp.where(low, vr[:mini], vr_swap[mini:])
        logits = jnp.where(lane_low(vr.shape), vr_swap, vr)
        logits = jnp.sum(logits * eye, axis=0, keepdims=True)
        rate = base_rate * jax.nn.sigmoid(logits + bias_ref[...]) / mini
        high = rate.astype(bf16).astype(f32)
        pad = jnp.zeros((PACK - 2, both), f32)
        at = base + i * (both + PACK)
        kv_ref[pl.ds(at, mini), :] = keys.astype(bf16)
        kv_ref[pl.ds(at + mini, mini), :] = values.astype(bf16)
        kv_ref[pl.ds(at + both, PACK), :] = jnp.concatenate([high, rate - high, pad], axis=0).astype(bf16)
        q_ref[pl.ds(i * mini, mini), :] = queries.astype(bf16)


def gelu_both(z):
    square = z * z
    tangent = jnp.tanh(z * (gelu_coef + (gelu_coef * gelu_cubic) * square))
    half = 0.5 * z
    value = half + half * tangent
    slope = (0.5 + 0.5 * tangent) + (half - half * (tangent * tangent)) * (
        gelu_coef + (3.0 * gelu_coef * gelu_cubic) * square
    )
    return value, slope


def gelu(z):
    tangent = jnp.tanh(z * (gelu_coef + (gelu_coef * gelu_cubic) * (z * z)))
    half = 0.5 * z
    return half + half * tangent


def chain_kernel(seq_count, ids_ref, *refs):
    kv_ref, refs = refs[0], refs[1:]
    q_early, q_late, gain_ref, bias_ref, w1_ref, b1_ref, w2_ref, b2_ref = refs[:8]
    out_ref, kv_s, q_s, w1_s, b1_s, w2_s, b2_s, z1_s = refs[8:]
    inner = w1_ref.shape[-1]
    both = gain_ref.shape[1] * 2
    d = both // 2
    mini = d
    minis = kv_s.shape[1]
    place, flip = ids_ref[0], ids_ref[1]
    gain = jnp.concatenate([gain_ref[...], gain_ref[...]], axis=1)
    bias = jnp.concatenate([bias_ref[...], bias_ref[...]], axis=1)
    gain_sq = gain * gain
    row_id = lax.broadcasted_iota(jnp.int32, (both, both), 0)
    lane_id = lax.broadcasted_iota(jnp.int32, (both, both), 1)
    same = ((row_id < mini) == (lane_id < mini)).astype(f32)
    causal = same * (row_id >= lane_id).astype(f32)
    ones = same.astype(bf16)
    pick = (
        lax.broadcasted_iota(jnp.int32, (mini, both), 0)
        == lax.rem(lax.broadcasted_iota(jnp.int32, (mini, both), 1), mini)
    ).astype(f32)

    def per_row(pair):
        return jnp.concatenate(
            [
                jnp.broadcast_to(pair[:1], (mini, inner)),
                jnp.broadcast_to(pair[1:], (mini, inner)),
            ],
            axis=0,
        )

    def halves(x):
        low = lane_low(x.shape)
        first = jnp.sum(jnp.where(low, x, 0.0), axis=1, keepdims=True)
        second = jnp.sum(jnp.where(low, 0.0, x), axis=1, keepdims=True)
        return jnp.concatenate([first, second], axis=0)

    def spread(col):
        low = lane_low((mini, both))
        return jnp.where(low, col[:mini], col[mini:])

    def keys_of(j, m):
        return kv_s[j, m, pl.ds(0, mini), :]

    def step(j, m, state, z1, kb, key_cat, nxt, query):
        w1, b1, w2, b2 = state
        w1h, (w2h, w2m, w2l) = w1.astype(bf16), thirds(w2)
        value_cat = kv_s[j, m, pl.ds(mini, mini), :].astype(f32)
        rate_rows = kv_s[j, m, pl.ds(both, PACK), :].astype(f32)
        e = halves(pick * (rate_rows[:1] + rate_rows[1:2]))
        u = gain * (bias - (value_cat - key_cat.astype(f32)))
        u_mean = halves(u) * (1.0 / d)

        x2, slope = gelu_both(z1)
        x2h, x2m, x2l = thirds(x2)
        pieces = dot(jnp.concatenate([x2h, x2m], axis=0), jnp.concatenate([w2h, w2m], axis=1))
        small = dot(x2h, w2l) + (dot(x2l, w2h) + pieces[both:, both:])
        medium = pieces[:both, both:] + pieces[both:, :both]
        z = lane_cat(pieces[:both, :both] + (medium + small)) + b2
        scaled = gain_sq * z
        rs = lax.rsqrt(halves(z * z) * (1.0 / d) + ln_eps)
        mean_g = rs * halves(scaled) * (1.0 / d) + u_mean
        mean_gn = rs * (rs * halves(scaled * z) + halves(u * z)) * (1.0 / d)
        alpha = e * rs
        pulled = dot(blocks(u), w2h, NT)
        back = dot(jnp.concatenate([blocks(scaled), blocks(z)], axis=0), w2h, NT)
        d1 = (alpha * rs) * (back[:both] - mean_gn * back[both:]) + alpha * pulled
        h1h = (d1 * slope).astype(bf16)
        h1 = h1h.astype(f32)
        h2 = spread(alpha) * ((gain_sq - spread(mean_gn)) * (spread(rs) * z) + (u - spread(mean_g)))
        h2h, h2m = (blocks(x) for x in halved(h2))

        z1_next, kb_next, result = None, None, None
        streams = [] if nxt is None else [blocks(nxt)]
        if query is not None:
            streams.append(blocks(query))
        streams = jnp.concatenate(streams, axis=0)
        against_keys = dot(streams, kb, NT)
        against_state = dot(streams, w1h)
        lhs = []
        if nxt is not None:
            kb_next = streams[:both]
            lhs += [(against_keys[:both] + same).astype(bf16)]
        if query is not None:
            lhs.append((causal * (against_keys[-both:] + 1.0)).astype(bf16))
        moved = dot(jnp.concatenate(lhs, axis=0), h1h)
        if nxt is not None:
            z1_next = against_state[:both] + per_row(b1) - moved[:both]
        if query is not None:
            first_bar = against_state[-both:] + per_row(b1) - moved[-both:]
            hidden_bar = gelu(first_bar).astype(bf16)
            attend_hidden = causal * (dot(hidden_bar, x2h, NT) + 1.0)
            zb = lane_cat(dot(hidden_bar, w2h) - dot(attend_hidden, h2h)) + b2
            var = spread(halves(zb * zb)) * (1.0 / d)
            result = query.astype(f32) + gain * (zb * lax.rsqrt(var + ln_eps)) + bias
            if nxt is None:
                return None, None, None, result

        w1 = w1 - dot(kb, h1h, TN)
        b1 = b1 - jnp.concatenate(
            [
                jnp.sum(h1[:mini], axis=0, keepdims=True),
                jnp.sum(h1[mini:], axis=0, keepdims=True),
            ],
            axis=0,
        )
        w2 = w2 - dot(
            jnp.concatenate([x2h, x2m, x2h], axis=0), jnp.concatenate([h2h, h2h, h2m], axis=0), TN
        )
        b2 = b2 - jnp.sum(h2, axis=0, keepdims=True)
        return (w1, b1, w2, b2), z1_next, kb_next, result

    for p in range(minis):
        at = pl.ds((p % (minis - 1)) * mini, mini)
        q_s[p ^ flip] = q_early[at, :] if p + 1 < minis else q_late[...]
    for j in range(seq_count):
        for p in range(minis):
            kv_s[j, p ^ flip] = kv_ref[j, pl.ds(p * (both + PACK), both + PACK), :]

    w2, b2 = w2_ref[0], b2_ref[...]
    w2 = w2 - jnp.mean(w2, axis=0, keepdims=True)
    b2 = b2 - jnp.mean(b2, axis=1, keepdims=True)
    w1_s[...] = jnp.concatenate([w1_ref[0], w1_ref[0]], axis=0)
    b1_s[...] = jnp.concatenate([b1_ref[...], b1_ref[...]], axis=0)
    w2_s[...] = jnp.concatenate([w2, w2], axis=0).T
    b2_s[...] = jnp.concatenate([b2, b2], axis=1)
    z1_s[...] = dot(blocks(keys_of(0, 0)), w1_s[...]) + per_row(b1_s[...])

    def segment(j, queries):
        state, z1 = (w1_s[...], b1_s[...], w2_s[...], b2_s[...]), z1_s[...]
        key_cat = keys_of(j, 0)
        kb = blocks(key_cat)
        for m in range(minis):
            if m + 1 < minis:
                nxt = keys_of(j, m + 1)
            else:
                nxt = None if queries else keys_of(j + 1, 0)
            query = q_s[m] if queries else None
            state, z1, kb, result = step(j, m, state, z1, kb, key_cat, nxt, query)
            if queries:
                out_ref[pl.ds(m * mini, mini), :] = result.astype(bf16)
            key_cat = nxt
        if not queries:
            w1_s[...], b1_s[...], w2_s[...], b2_s[...] = state
            z1_s[...] = z1

    def body(j, carry):
        segment(j, False)
        return carry

    lax.fori_loop(0, place, body, 0)
    segment(place, True)


def out_kernel(count, ids_ref, heads_ref, *refs):
    w_refs, (out_ref, w_s, out_s, sems) = refs[:count], refs[count:]
    heads, rows, both = heads_ref.shape
    d = both // 2
    low = lane_low((rows, both))
    me = 2 * ids_ref[1] + ids_ref[2]
    order = list(range(heads)) if count == 1 else [me ^ i for i in range(heads)]
    firsts, seconds = [], []
    for h in range(0, heads, 2):
        even, odd = heads_ref[order[h]].astype(f32), heads_ref[order[h + 1]].astype(f32)
        firsts.append(jnp.where(low, even, pltpu.roll(odd, d, 1)))
        seconds.append(jnp.where(low, pltpu.roll(even, d, 1), odd))
    lhs = jnp.concatenate(
        [jnp.concatenate(firsts, axis=1), jnp.concatenate(seconds, axis=1)], axis=0
    )
    share = d // 4
    for i in range(2 if count > 1 else 0):
        for flip in range(4):
            at = pl.multiple_of(i * d + (ids_ref[0] ^ flip) * share, share)
            w_s[pl.ds(at, share), :] = w_refs[count - 2 + i][pl.ds(flip * share, share), :]
    whole = w_refs if count == 1 else [*w_refs[:-2], w_s]
    cols = out_s.shape[3]
    copies = []
    for c in range(out_s.shape[0]):
        lanes = slice(c * cols, (c + 1) * cols)
        prod = dot(lhs, jnp.concatenate([w[:, lanes] for w in whole], axis=0)).astype(bf16)
        out_s[c, 0] = prod[:rows]
        out_s[c, 1] = prod[rows:]
        copies.append(pltpu.make_async_copy(out_s.at[c], out_ref.at[:, :, lanes], sems.at[c]))
        copies[-1].start()
    for copy in copies:
        copy.wait()


def swapped(array, flip, axis="row"):
    return lax.ppermute(array, axis, [(i, i ^ flip) for i in range(lax.axis_size(axis))])


VMEM_LIMIT = 14 * 1024 * 1024


def on_device(
    tokens,
    w_qkv,
    w_rate,
    rate_bias,
    w_out,
    w_first_init,
    b_first_init,
    w_second_init,
    b_second_init,
    ln_gain,
    ln_bias,
):
    videos, tok_part, width = tokens.shape
    d = w_qkv.shape[0] // 3
    both = 2 * d
    row_count, seq_count = lax.axis_size("row"), lax.axis_size("seq")
    minis = tok_part * row_count // MINI
    paired = row_count == 8 and minis == 4 and seq_count == 4
    vmem = pl.BlockSpec(memory_space=pltpu.VMEM)
    smem = pl.BlockSpec(memory_space=pltpu.SMEM)
    params = pltpu.CompilerParams(vmem_limit_bytes=VMEM_LIMIT)
    row = lax.axis_index("row") if paired else 0
    ids = jnp.stack([lax.axis_index("seq"), row // 2, row % 2]).astype(jnp.int32)
    bias = rate_bias.reshape(1, 1)

    def project(count, pieces, first, parts, weights, *before):
        rows = count * MINI
        total = count if first else minis
        out_shape = [
            jax.ShapeDtypeStruct((total * (2 * MINI + PACK), both), bf16),
            jax.ShapeDtypeStruct((rows, both), bf16),
        ]
        if first:
            out_shape.append(jax.ShapeDtypeStruct((4 * d, width), bf16))
        return pl.pallas_call(
            partial(project_kernel, count, pieces, first),
            out_shape=out_shape,
            in_specs=[smem] + [vmem] * (len(parts) + len(weights) + 1 + len(before)),
            out_specs=[vmem] * len(out_shape),
            scratch_shapes=[pltpu.VMEM((2 * rows, 4 * d), f32)],
            compiler_params=params,
            cost_estimate=pl.CostEstimate(
                flops=16 * rows * d * width, bytes_accessed=4_000_000, transcendentals=0
            ),
            name="project" if first else "finish",
        )(ids, *parts, *weights, bias, *before)

    if paired:
        share = w_out.shape[0] // seq_count
        place = lax.axis_index("seq")
        far, near = swapped(tokens, 4), swapped(tokens, 2)
        own, w_own = swapped(tokens, 1), swapped(w_out, 1)
        w_share = lax.dynamic_slice_in_dim(w_out, place * share, share, 0)
        w_share = swapped(w_share, 6)
        far, near, own, w_own, w_share = lax.optimization_barrier((far, near, own, w_own, w_share))
        last = swapped(far, 2)
        near_other, far_other = swapped(near, 1), swapped(far, 1)
        w_end = [w_share] + [swapped(w_share, flip, "seq") for flip in range(1, seq_count)]
        early = [tokens, own, near, near_other, far, far_other]
        kv_early, q_early, stack = project(3, 2, True, early, (w_qkv, w_rate))
        last, kv_early, *w_end = lax.optimization_barrier((last, kv_early, *w_end))
        w_end = jnp.concatenate(w_end, axis=0)
        late = [last, swapped(last, 1)]
        w_after, _ = lax.optimization_barrier((w_out, last))
        w_near, w_far = swapped(w_after, 2), swapped(w_after, 4)
        kv, q_late = project(1, 2, False, late, (stack,), kv_early)
    else:
        whole = lax.all_gather(tokens, "row", axis=1, tiled=True)
        whole = whole.reshape(videos, minis, MINI, width)
        parts = [whole[:, m] for m in range(minis)]
        kv_early, q_early, stack = project(minis - 1, 1, True, parts[:-1], (w_qkv, w_rate))
        kv, q_late = project(1, 1, False, parts[-1:], (stack,), kv_early)
        w_parts = [lax.all_gather(w_out, "row", axis=0, tiled=True)]

    inner = w_first_init.shape[2]
    operands = [lax.all_gather(kv, "seq"), q_early, q_late, ln_gain, ln_bias]
    operands += [w_first_init, b_first_init]
    operands += [jnp.swapaxes(w_second_init, 1, 2), b_second_init]
    heads = pl.pallas_call(
        partial(chain_kernel, seq_count),
        out_shape=jax.ShapeDtypeStruct((minis * MINI, both), bf16),
        in_specs=[smem] + [vmem] * len(operands),
        out_specs=vmem,
        scratch_shapes=[
            pltpu.VMEM((seq_count, minis, 2 * MINI + PACK, both), bf16),
            pltpu.VMEM((minis, MINI, both), bf16),
            pltpu.VMEM((both, inner), f32),
            pltpu.VMEM((2, inner), f32),
            pltpu.VMEM((inner, both), f32),
            pltpu.VMEM((1, both), f32),
            pltpu.VMEM((2 * MINI, inner), f32),
        ],
        compiler_params=params,
        name="chain",
    )(ids, *operands)
    if paired:
        w_near, w_far, w_end, _ = lax.optimization_barrier((w_near, w_far, w_end, heads))
        w_parts = [w_out, w_own] + [x for w in (w_near, w_far, w_end) for x in (w, swapped(w, 1))]
    heads = heads.reshape(row_count, tok_part, both)
    arrived = lax.all_to_all(heads, "row", split_axis=0, concat_axis=0, tiled=True)
    return pl.pallas_call(
        partial(out_kernel, len(w_parts)),
        out_shape=jax.ShapeDtypeStruct((videos, tok_part, width), bf16),
        in_specs=[smem, vmem] + [vmem] * len(w_parts),
        out_specs=pl.BlockSpec(memory_space=pl.ANY),
        scratch_shapes=[
            pltpu.VMEM((2 * d, width), bf16),
            pltpu.VMEM((MIX_CHUNKS, videos, tok_part, width // MIX_CHUNKS), bf16),
            pltpu.SemaphoreType.DMA((MIX_CHUNKS,)),
        ],
        compiler_params=params,
        name="mix",
    )(ids, arrived, *w_parts)


def solution(mesh):
    in_specs = (
        P(None, ("seq", "row"), None),
        P("row", None),
        P("row", None),
        P("row"),
        P("row", None),
        P("row", None, None),
        P("row", None),
        P("row", None, None),
        P("row", None),
        P("row", None),
        P("row", None),
    )
    out_specs = P(None, ("seq", "row"), None)
    return jax.shard_map(
        on_device, mesh=mesh, in_specs=in_specs, out_specs=out_specs, check_vma=False
    )
```

```python
from functools import partial

import jax
import jax.numpy as jnp
from jax import lax
from jax.experimental import pallas as pl
from jax.experimental.pallas import tpu as pltpu
from jax.sharding import PartitionSpec as P

MINI = 64
gelu_coef = 0.7978845608028654
gelu_cubic = 0.044715
base_rate = 0.01
ln_eps = 1e-06

f32 = jnp.float32
bf16 = jnp.bfloat16
NN = ((1,), (0,))
NT = ((1,), (1,))
TN = ((0,), (0,))


def dot(left, right, dims=NN):
    return lax.dot_general(
        left.astype(bf16), right.astype(bf16), (dims, ((), ())), preferred_element_type=f32
    )


def halved(x):
    high = x.astype(bf16)
    return high, (x - high.astype(f32)).astype(bf16)


def thirds(x):
    high = x.astype(bf16)
    rest = x - high.astype(f32)
    middle = rest.astype(bf16)
    return high, middle, (rest - middle.astype(f32)).astype(bf16)


def lane_low(shape):
    return lax.broadcasted_iota(jnp.int32, shape, len(shape) - 1) < shape[-1] // 2


def blocks(cat):
    low = lane_low(cat.shape)
    zero = jnp.zeros_like(cat)
    return jnp.concatenate([jnp.where(low, cat, zero), jnp.where(low, zero, cat)], axis=0)


def lane_cat(rows):
    half = rows.shape[0] // 2
    return jnp.where(lane_low((half, rows.shape[1])), rows[:half], rows[half:])


PACK = 16
MIX_CHUNKS = 4


def project_kernel(count, pieces, first, ids_ref, *refs):
    x_refs, refs = refs[: count * pieces], refs[count * pieces :]
    if first:
        w_ref, wr_ref, bias_ref, kv_ref, q_ref, stack_ref, prod_s = refs
        d, base = w_ref.shape[0] // 3, 0
        stack_ref[: 3 * d, :] = w_ref[...]
        stack_ref[3 * d :, :] = jnp.broadcast_to(wr_ref[...], (d, wr_ref.shape[1]))
    else:
        stack_ref, bias_ref, early_ref, kv_ref, q_ref, prod_s = refs
        d = stack_ref.shape[0] // 4
        base = early_ref.shape[0]
        kv_ref[:base, :] = early_ref[...]
    mini = d
    both = 2 * mini
    part = x_refs[0].shape[1]
    x = jnp.concatenate([x_ref[...].reshape(-1, x_ref.shape[2]) for x_ref in x_refs], axis=0)
    prod = dot(x, stack_ref[...], NT)
    core = ids_ref[2]
    for i in range(count):
        for j in range(pieces):
            where = (core if j == 0 else 1 - core) * part if pieces > 1 else 0
            for video in range(2):
                row = ((i * pieces + j) * 2 + video) * part
                spot = i * both + video * mini + where
                if pieces > 1:
                    spot = pl.multiple_of(spot, part)
                prod_s[pl.ds(spot, part), :] = prod[row : row + part]
    eye = (
        lax.broadcasted_iota(jnp.int32, (both, both), 0)
        == lax.broadcasted_iota(jnp.int32, (both, both), 1)
    ).astype(f32)
    low = lane_low((mini, 2 * d))
    for i in range(count):
        prod = prod_s[pl.ds(i * both, both), :]
        qk, vr = prod[:, : 2 * d], prod[:, 2 * d :]
        qk_swap, vr_swap = pltpu.roll(qk, d, 1), pltpu.roll(vr, d, 1)
        keys = jnp.where(low, qk_swap[:mini], qk[mini:])
        queries = jnp.where(low, qk[:mini], qk_swap[mini:])
        values = jnp.where(low, vr[:mini], vr_swap[mini:])
        logits = jnp.where(lane_low(vr.shape), vr_swap, vr)
        logits = jnp.sum(logits * eye, axis=0, keepdims=True)
        rate = base_rate * jax.nn.sigmoid(logits + bias_ref[...]) / mini
        high = rate.astype(bf16).astype(f32)
        pad = jnp.zeros((PACK - 2, both), f32)
        at = base + i * (both + PACK)
        kv_ref[pl.ds(at, mini), :] = keys.astype(bf16)
        kv_ref[pl.ds(at + mini, mini), :] = values.astype(bf16)
        kv_ref[pl.ds(at + both, PACK), :] = jnp.concatenate([high, rate - high, pad], axis=0).astype(bf16)
        q_ref[pl.ds(i * mini, mini), :] = queries.astype(bf16)


def gelu_both(z):
    square = z * z
    tangent = jnp.tanh(z * (gelu_coef + (gelu_coef * gelu_cubic) * square))
    half = 0.5 * z
    value = half + half * tangent
    slope = (0.5 + 0.5 * tangent) + (half - half * (tangent * tangent)) * (
        gelu_coef + (3.0 * gelu_coef * gelu_cubic) * square
    )
    return value, slope


def gelu(z):
    tangent = jnp.tanh(z * (gelu_coef + (gelu_coef * gelu_cubic) * (z * z)))
    half = 0.5 * z
    return half + half * tangent


def chain_kernel(seq_count, ids_ref, *refs):
    kv_ref, refs = refs[0], refs[1:]
    q_early, q_late, gain_ref, bias_ref, w1_ref, b1_ref, w2_ref, b2_ref = refs[:8]
    out_ref, kv_s, q_s, w1_s, b1_s, w2_s, b2_s, z1_s = refs[8:]
    inner = w1_ref.shape[-1]
    both = gain_ref.shape[1] * 2
    d = both // 2
    mini = d
    minis = kv_s.shape[1]
    place, flip = ids_ref[0], ids_ref[1]
    gain = jnp.concatenate([gain_ref[...], gain_ref[...]], axis=1)
    bias = jnp.concatenate([bias_ref[...], bias_ref[...]], axis=1)
    gain_sq = gain * gain
    row_id = lax.broadcasted_iota(jnp.int32, (both, both), 0)
    lane_id = lax.broadcasted_iota(jnp.int32, (both, both), 1)
    same = ((row_id < mini) == (lane_id < mini)).astype(f32)
    causal = same * (row_id >= lane_id).astype(f32)
    ones = same.astype(bf16)
    pick = (
        lax.broadcasted_iota(jnp.int32, (mini, both), 0)
        == lax.rem(lax.broadcasted_iota(jnp.int32, (mini, both), 1), mini)
    ).astype(f32)

    def per_row(pair):
        return jnp.concatenate(
            [
                jnp.broadcast_to(pair[:1], (mini, inner)),
                jnp.broadcast_to(pair[1:], (mini, inner)),
            ],
            axis=0,
        )

    def halves(x):
        low = lane_low(x.shape)
        first = jnp.sum(jnp.where(low, x, 0.0), axis=1, keepdims=True)
        second = jnp.sum(jnp.where(low, 0.0, x), axis=1, keepdims=True)
        return jnp.concatenate([first, second], axis=0)

    def spread(col):
        low = lane_low((mini, both))
        return jnp.where(low, col[:mini], col[mini:])

    def keys_of(j, m):
        return kv_s[j, m, pl.ds(0, mini), :]

    def step(j, m, state, z1, kb, key_cat, nxt, query):
        w1, b1, w2, b2 = state
        w1h, (w2h, w2m, w2l) = w1.astype(bf16), thirds(w2)
        value_cat = kv_s[j, m, pl.ds(mini, mini), :].astype(f32)
        rate_rows = kv_s[j, m, pl.ds(both, PACK), :].astype(f32)
        e = halves(pick * (rate_rows[:1] + rate_rows[1:2]))
        u = gain * (bias - (value_cat - key_cat.astype(f32)))
        u_mean = halves(u) * (1.0 / d)

        x2, slope = gelu_both(z1)
        x2h, x2m, x2l = thirds(x2)
        pieces = dot(jnp.concatenate([x2h, x2m], axis=0), jnp.concatenate([w2h, w2m], axis=1))
        small = lane_cat(dot(x2h, w2l)) + (lane_cat(dot(x2l, w2h)) + lane_cat(pieces[both:, both:]))
        medium = lane_cat(pieces[:both, both:]) + lane_cat(pieces[both:, :both])
        z = lane_cat(pieces[:both, :both]) + (medium + (small + b2))
        scaled = gain_sq * z
        rs = lax.rsqrt(halves(z * z) * (1.0 / d) + ln_eps)
        mean_g = rs * halves(scaled) * (1.0 / d) + u_mean
        mean_gn = rs * (rs * halves(scaled * z) + halves(u * z)) * (1.0 / d)
        alpha = e * rs
        pulled = dot(blocks(u), w2h, NT)
        back = dot(jnp.concatenate([blocks(scaled), blocks(z)], axis=0), w2h, NT)
        d1 = (alpha * rs) * (back[:both] - mean_gn * back[both:]) + alpha * pulled
        h1h = (d1 * slope).astype(bf16)
        h1 = h1h.astype(f32)
        h2 = spread(alpha) * ((gain_sq - spread(mean_gn)) * (spread(rs) * z) + (u - spread(mean_g)))
        h2h, h2m = (blocks(x) for x in halved(h2))

        z1_next, kb_next, result = None, None, None
        streams = [] if nxt is None else [blocks(nxt)]
        if query is not None:
            streams.append(blocks(query))
        streams = jnp.concatenate(streams, axis=0)
        against_keys = dot(streams, kb, NT)
        against_state = dot(streams, w1h)
        lhs = []
        if nxt is not None:
            kb_next = streams[:both]
            lhs += [(against_keys[:both] + same).astype(bf16)]
        if query is not None:
            lhs.append((causal * (against_keys[-both:] + 1.0)).astype(bf16))
        moved = dot(jnp.concatenate(lhs, axis=0), h1h)
        if nxt is not None:
            z1_next = against_state[:both] + per_row(b1) - moved[:both]
        if query is not None:
            first_bar = against_state[-both:] + per_row(b1) - moved[-both:]
            hidden_bar = gelu(first_bar).astype(bf16)
            attend_hidden = causal * (dot(hidden_bar, x2h, NT) + 1.0)
            zb = lane_cat(dot(hidden_bar, w2h) - dot(attend_hidden, h2h)) + b2
            var = spread(halves(zb * zb)) * (1.0 / d)
            result = query.astype(f32) + gain * (zb * lax.rsqrt(var + ln_eps)) + bias
            if nxt is None:
                return None, None, None, result

        w1 = w1 - dot(kb, h1h, TN)
        b1 = b1 - jnp.concatenate(
            [
                jnp.sum(h1[:mini], axis=0, keepdims=True),
                jnp.sum(h1[mini:], axis=0, keepdims=True),
            ],
            axis=0,
        )
        w2 = w2 - dot(
            jnp.concatenate([x2h, x2m, x2h], axis=0), jnp.concatenate([h2h, h2h, h2m], axis=0), TN
        )
        b2 = b2 - jnp.sum(h2, axis=0, keepdims=True)
        return (w1, b1, w2, b2), z1_next, kb_next, result

    for p in range(minis):
        at = pl.ds((p % (minis - 1)) * mini, mini)
        q_s[p ^ flip] = q_early[at, :] if p + 1 < minis else q_late[...]
    for j in range(seq_count):
        for p in range(minis):
            kv_s[j, p ^ flip] = kv_ref[j, pl.ds(p * (both + PACK), both + PACK), :]

    w2, b2 = w2_ref[0], b2_ref[...]
    w2 = w2 - jnp.mean(w2, axis=0, keepdims=True)
    b2 = b2 - jnp.mean(b2, axis=1, keepdims=True)
    w1_s[...] = jnp.concatenate([w1_ref[0], w1_ref[0]], axis=0)
    b1_s[...] = jnp.concatenate([b1_ref[...], b1_ref[...]], axis=0)
    w2_s[...] = jnp.concatenate([w2, w2], axis=0).T
    b2_s[...] = jnp.concatenate([b2, b2], axis=1)
    z1_s[...] = dot(blocks(keys_of(0, 0)), w1_s[...]) + per_row(b1_s[...])

    def segment(j, queries):
        state, z1 = (w1_s[...], b1_s[...], w2_s[...], b2_s[...]), z1_s[...]
        key_cat = keys_of(j, 0)
        kb = blocks(key_cat)
        for m in range(minis):
            if m + 1 < minis:
                nxt = keys_of(j, m + 1)
            else:
                nxt = None if queries else keys_of(j + 1, 0)
            query = q_s[m] if queries else None
            state, z1, kb, result = step(j, m, state, z1, kb, key_cat, nxt, query)
            if queries:
                out_ref[pl.ds(m * mini, mini), :] = result.astype(bf16)
            key_cat = nxt
        if not queries:
            w1_s[...], b1_s[...], w2_s[...], b2_s[...] = state
            z1_s[...] = z1

    def body(j, carry):
        segment(j, False)
        return carry

    lax.fori_loop(0, place, body, 0)
    segment(place, True)


def out_kernel(count, ids_ref, heads_ref, *refs):
    w_refs, (out_ref, w_s, out_s, sems) = refs[:count], refs[count:]
    heads, rows, both = heads_ref.shape
    d = both // 2
    low = lane_low((rows, both))
    me = 2 * ids_ref[1] + ids_ref[2]
    order = list(range(heads)) if count == 1 else [me ^ i for i in range(heads)]
    firsts, seconds = [], []
    for h in range(0, heads, 2):
        even, odd = heads_ref[order[h]].astype(f32), heads_ref[order[h + 1]].astype(f32)
        firsts.append(jnp.where(low, even, pltpu.roll(odd, d, 1)))
        seconds.append(jnp.where(low, pltpu.roll(even, d, 1), odd))
    lhs = jnp.concatenate(
        [jnp.concatenate(firsts, axis=1), jnp.concatenate(seconds, axis=1)], axis=0
    )
    share = d // 4
    for i in range(2 if count > 1 else 0):
        for flip in range(4):
            at = pl.multiple_of(i * d + (ids_ref[0] ^ flip) * share, share)
            w_s[pl.ds(at, share), :] = w_refs[count - 2 + i][pl.ds(flip * share, share), :]
    whole = w_refs if count == 1 else [*w_refs[:-2], w_s]
    cols = out_s.shape[3]
    copies = []
    for c in range(out_s.shape[0]):
        lanes = slice(c * cols, (c + 1) * cols)
        prod = dot(lhs, jnp.concatenate([w[:, lanes] for w in whole], axis=0)).astype(bf16)
        out_s[c, 0] = prod[:rows]
        out_s[c, 1] = prod[rows:]
        copies.append(pltpu.make_async_copy(out_s.at[c], out_ref.at[:, :, lanes], sems.at[c]))
        copies[-1].start()
    for copy in copies:
        copy.wait()


def swapped(array, flip, axis="row"):
    return lax.ppermute(array, axis, [(i, i ^ flip) for i in range(lax.axis_size(axis))])


VMEM_LIMIT = 14 * 1024 * 1024


def on_device(
    tokens,
    w_qkv,
    w_rate,
    rate_bias,
    w_out,
    w_first_init,
    b_first_init,
    w_second_init,
    b_second_init,
    ln_gain,
    ln_bias,
):
    videos, tok_part, width = tokens.shape
    d = w_qkv.shape[0] // 3
    both = 2 * d
    row_count, seq_count = lax.axis_size("row"), lax.axis_size("seq")
    minis = tok_part * row_count // MINI
    paired = row_count == 8 and minis == 4 and seq_count == 4
    vmem = pl.BlockSpec(memory_space=pltpu.VMEM)
    smem = pl.BlockSpec(memory_space=pltpu.SMEM)
    params = pltpu.CompilerParams(vmem_limit_bytes=VMEM_LIMIT)
    row = lax.axis_index("row") if paired else 0
    ids = jnp.stack([lax.axis_index("seq"), row // 2, row % 2]).astype(jnp.int32)
    bias = rate_bias.reshape(1, 1)

    def project(count, pieces, first, parts, weights, *before):
        rows = count * MINI
        total = count if first else minis
        out_shape = [
            jax.ShapeDtypeStruct((total * (2 * MINI + PACK), both), bf16),
            jax.ShapeDtypeStruct((rows, both), bf16),
        ]
        if first:
            out_shape.append(jax.ShapeDtypeStruct((4 * d, width), bf16))
        return pl.pallas_call(
            partial(project_kernel, count, pieces, first),
            out_shape=out_shape,
            in_specs=[smem] + [vmem] * (len(parts) + len(weights) + 1 + len(before)),
            out_specs=[vmem] * len(out_shape),
            scratch_shapes=[pltpu.VMEM((2 * rows, 4 * d), f32)],
            compiler_params=params,
            cost_estimate=pl.CostEstimate(
                flops=16 * rows * d * width, bytes_accessed=4_000_000, transcendentals=0
            ),
            name="project" if first else "finish",
        )(ids, *parts, *weights, bias, *before)

    if paired:
        share = w_out.shape[0] // seq_count
        place = lax.axis_index("seq")
        far, near = swapped(tokens, 4), swapped(tokens, 2)
        own, w_own = swapped(tokens, 1), swapped(w_out, 1)
        w_share = lax.dynamic_slice_in_dim(w_out, place * share, share, 0)
        w_share = swapped(w_share, 6)
        far, near, own, w_own, w_share = lax.optimization_barrier((far, near, own, w_own, w_share))
        last = swapped(far, 2)
        near_other, far_other = swapped(near, 1), swapped(far, 1)
        w_end = [w_share] + [swapped(w_share, flip, "seq") for flip in range(1, seq_count)]
        early = [tokens, own, near, near_other, far, far_other]
        kv_early, q_early, stack = project(3, 2, True, early, (w_qkv, w_rate))
        last, kv_early, *w_end = lax.optimization_barrier((last, kv_early, *w_end))
        w_end = jnp.concatenate(w_end, axis=0)
        late = [last, swapped(last, 1)]
        w_after, _ = lax.optimization_barrier((w_out, last))
        w_near, w_far = swapped(w_after, 2), swapped(w_after, 4)
        kv, q_late = project(1, 2, False, late, (stack,), kv_early)
    else:
        whole = lax.all_gather(tokens, "row", axis=1, tiled=True)
        whole = whole.reshape(videos, minis, MINI, width)
        parts = [whole[:, m] for m in range(minis)]
        kv_early, q_early, stack = project(minis - 1, 1, True, parts[:-1], (w_qkv, w_rate))
        kv, q_late = project(1, 1, False, parts[-1:], (stack,), kv_early)
        w_parts = [lax.all_gather(w_out, "row", axis=0, tiled=True)]

    inner = w_first_init.shape[2]
    operands = [lax.all_gather(kv, "seq"), q_early, q_late, ln_gain, ln_bias]
    operands += [w_first_init, b_first_init]
    operands += [jnp.swapaxes(w_second_init, 1, 2), b_second_init]
    heads = pl.pallas_call(
        partial(chain_kernel, seq_count),
        out_shape=jax.ShapeDtypeStruct((minis * MINI, both), bf16),
        in_specs=[smem] + [vmem] * len(operands),
        out_specs=vmem,
        scratch_shapes=[
            pltpu.VMEM((seq_count, minis, 2 * MINI + PACK, both), bf16),
            pltpu.VMEM((minis, MINI, both), bf16),
            pltpu.VMEM((both, inner), f32),
            pltpu.VMEM((2, inner), f32),
            pltpu.VMEM((inner, both), f32),
            pltpu.VMEM((1, both), f32),
            pltpu.VMEM((2 * MINI, inner), f32),
        ],
        compiler_params=params,
        name="chain",
    )(ids, *operands)
    if paired:
        w_near, w_far, w_end, _ = lax.optimization_barrier((w_near, w_far, w_end, heads))
        w_parts = [w_out, w_own] + [x for w in (w_near, w_far, w_end) for x in (w, swapped(w, 1))]
    heads = heads.reshape(row_count, tok_part, both)
    arrived = lax.all_to_all(heads, "row", split_axis=0, concat_axis=0, tiled=True)
    return pl.pallas_call(
        partial(out_kernel, len(w_parts)),
        out_shape=jax.ShapeDtypeStruct((videos, tok_part, width), bf16),
        in_specs=[smem, vmem] + [vmem] * len(w_parts),
        out_specs=pl.BlockSpec(memory_space=pl.ANY),
        scratch_shapes=[
            pltpu.VMEM((2 * d, width), bf16),
            pltpu.VMEM((MIX_CHUNKS, videos, tok_part, width // MIX_CHUNKS), bf16),
            pltpu.SemaphoreType.DMA((MIX_CHUNKS,)),
        ],
        compiler_params=params,
        name="mix",
    )(ids, arrived, *w_parts)


def solution(mesh):
    in_specs = (
        P(None, ("seq", "row"), None),
        P("row", None),
        P("row", None),
        P("row"),
        P("row", None),
        P("row", None, None),
        P("row", None),
        P("row", None, None),
        P("row", None),
        P("row", None),
        P("row", None),
    )
    out_specs = P(None, ("seq", "row"), None)
    return jax.shard_map(
        on_device, mesh=mesh, in_specs=in_specs, out_specs=out_specs, check_vma=False
    )
```
